512 devices in a mesh: elem: 64 (over z_hi, y, core), rhs: 8 (over z_lo, x).
Axes of the slice: x: 4, y: 8, z: 8 (z_hi: 4, z_lo: 2; z = z_hi * 2 + z_lo), core: 2. Of those that a mesh axis runs over, the one named last changes fastest.
Arguments:
- blocks: bfloat16 [262144, 448], P('elem'), may hold values from -0.25 to 0.25
- cols: int32 [6, 4096], P(None, 'elem'), may hold values from 0 to 4095, as said below
- inverse: bfloat16 [64, 262144], P(None, 'elem'), may hold values from -0.75 to 0.75
- right_side: float32 [128, 262144], P('rhs', 'elem'), may hold values from -6 to 6
- start: float32 [128, 262144], P('rhs', 'elem'), may hold values from -6 to 6
Outputs:
- adjoint: float32 [128, 262144], P('rhs', 'elem')
- residual: float32 [128, 262144], P('rhs', 'elem')
The draws below stay inside these ranges and needn't reach their ends.
Inputs may be any that keep to these rules, and one draw needn't show every extreme that they name: Element e lies on device e // 64 along elem; every element named by cols lies on a device at most 2 positions away from the device of the element whose face it is.
All inputs are finite; a program needn't handle non-finite values.
Results may differ from the reference program's by a relative error of at most 0.0036.
Values sent between devices are 32-bit elements; how exact they have to be, the bound alone decides.
No kernel may reach another device: no remote copies, remote signals or barrier semaphores. Data moves between devices by JAX's collectives and lax.ppermute only.
A program may use at most 64 MiB of HBM per device.

```python
import jax
import jax.numpy as jnp
from jax import lax

DOF = 64
SLOTS = 7
ELEM_DEV = 64
ELEMENTS = 4096
RHS = 128


def draw_cols(key, part):
    key = jax.random.fold_in(key, 11)
    first_key, second_key = jax.random.split(key)
    owner = jnp.arange(ELEMENTS, dtype=jnp.int32) // ELEM_DEV
    offsets = jax.random.randint(first_key, (6, ELEMENTS), -2, 3).astype(jnp.int32)
    device = jnp.clip(owner[None, :] + offsets, 0, ELEMENTS // ELEM_DEV - 1)
    within = jax.random.randint(second_key, (6, ELEMENTS), 0, ELEM_DEV).astype(jnp.int32)
    return (device * ELEM_DEV + within).astype(jnp.int32)


def steps_of(stream_key, shape, cuts, smallest, top_value):
    level = 1.0
    for dim, blocks in cuts:
        heights = jax.random.uniform(jax.random.fold_in(jax.random.fold_in(stream_key, 6), dim), (blocks,), jnp.float32, smallest / len(cuts), top_value / len(cuts))
        level = level * jnp.repeat(jnp.exp(heights), shape[dim] // blocks).reshape((-1,) + (1,) * (len(shape) - 1 - dim))
    return level


def centred(key, dims, scale, reach, pieces=(), held_as=jnp.bfloat16):
    drawn = scale * jax.random.normal(key, dims, jnp.float32)
    if pieces:
        drawn = drawn * steps_of(key, dims, pieces, -0.22, 0.18)
    return jnp.clip(drawn, -reach, reach).astype(held_as)


def setup_inputs(seed: int = 0) -> dict:
    splits = jax.random.split(jax.random.key(seed), 6)
    blocks = centred(splits[0], (ELEMENTS * DOF, SLOTS * DOF), (SLOTS * DOF) ** -0.5, 0.25, ((0, 64),))
    cols = draw_cols(jax.random.fold_in(splits[5], 71), 0)
    inverse = centred(splits[2], (DOF, ELEMENTS * DOF), DOF ** -0.5, 0.75, ((1, 64),))
    right_side = centred(splits[3], (RHS, ELEMENTS * DOF), 1.0, 6.0, ((0, 8), (1, 64)), jnp.float32)
    start = centred(splits[4], (RHS, ELEMENTS * DOF), 1.0, 6.0, ((0, 8), (1, 64)), jnp.float32)
    return {"blocks": blocks, "cols": cols, "inverse": inverse, "right_side": right_side, "start": start}


def transposed_apply(vector, blocks, cols):
    count = cols.shape[1]
    groups = count // ELEM_DEV
    width = vector.shape[0]
    vb = vector.astype(jnp.bfloat16).reshape(width, groups, ELEM_DEV, DOF).transpose(1, 0, 2, 3)
    panel = blocks.reshape(groups, ELEM_DEV, DOF, SLOTS * DOF)
    target = jnp.concatenate([jnp.arange(count, dtype=jnp.int32)[:, None], cols.T.astype(jnp.int32)], 1)
    target = target.reshape(groups, ELEM_DEV * SLOTS)

    def step(total, item):
        pan, piece, tgt = item
        terms = jnp.einsum('ikm,rik->rim', pan.astype(jnp.float32), piece.astype(jnp.float32))
        terms = terms.reshape(width, ELEM_DEV * SLOTS, DOF)
        return total.at[:, tgt, :].add(terms), None

    total, unused = lax.scan(step, jnp.zeros((width, count, DOF), jnp.float32), (panel, vb, target))
    return total.reshape(width, count * DOF)


def precondition(res, inverse):
    width = res.shape[0]
    count = inverse.shape[1] // DOF
    resb = res.astype(jnp.bfloat16).reshape(width, count, DOF).astype(jnp.float32)
    inv = inverse.reshape(DOF, count, DOF).astype(jnp.float32)
    return jnp.einsum('jik,rik->rij', inv, resb).reshape(width, count * DOF)


def reference(blocks, cols, inverse, right_side, start):
    res_one = right_side - transposed_apply(start, blocks, cols)
    first = start + precondition(res_one, inverse)
    residual = right_side - transposed_apply(first, blocks, cols)
    adjoint = first + precondition(residual, inverse)
    return adjoint, residual
```

```python
import functools

import jax
import jax.numpy as jnp
from jax import lax
from jax.experimental import pallas as pl
from jax.experimental.pallas import tpu as pltpu
from jax.sharding import PartitionSpec as P

DOF = 64
SLOTS = 7
QUAD = 4 * DOF
WINDOWS = 2
CHUNKS = 4


def masked_lanes(value, part):
    lane = lax.broadcasted_iota(jnp.int32, value.shape, 1)
    return jnp.where(lane // DOF == part, value, jnp.zeros_like(value))


def products(vb, panel):
    spread = jnp.concatenate([masked_lanes(vb, e) for e in range(4)], 0)
    return lax.dot_general(spread, panel, (((1,), (1,)), ((), ())), preferred_element_type=jnp.float32)


def scatter(vb_ref, panel_of, cols_ref, device, windows, own_ref, stage_ref):
    width = vb_ref.shape[0]
    count = cols_ref.shape[1]
    half = count // 2
    sign = 1 - 2 * lax.rem(device, 2)
    lane = lax.broadcasted_iota(jnp.int32, (width, 2 * DOF), 1) // DOF
    for window in windows:
        window[...] = jnp.zeros_like(window)
    for quad in range(count // 4):
        out = products(vb_ref[:, quad * QUAD : (quad + 1) * QUAD], panel_of(quad))
        stage = stage_ref.at[quad % 2]
        stage[:, : SLOTS * DOF] = out
        for e in range(4):
            element = 4 * quad + e
            rows = slice(e * width, (e + 1) * width)
            for s in range(1, SLOTS):
                tile = stage[rows, (s // 2) * 2 * DOF : (s // 2 + 1) * 2 * DOF]
                target = cols_ref[s - 1, element]
                role = sign * (target // count - device) + 2
                place = role * half + lax.rem(target, count) // 2
                side = lax.rem(target, 2)
                turned = pltpu.roll(tile, (side ^ (s % 2)) * DOF, 1)
                window = windows[s % len(windows)]
                window[place] += jnp.where(lane == side, turned, 0.0)
        for pair in range(2):
            low = stage[2 * pair * width : (2 * pair + 1) * width, : 2 * DOF]
            high = stage[(2 * pair + 1) * width : (2 * pair + 2) * width, : 2 * DOF]
            own_ref[2 * quad + pair] = jnp.where(lane == 0, low, pltpu.roll(high, DOF, 1))


def hand_out(windows, own_ref, far_ref, near_ref, here_ref, mate_ref):
    half = own_ref.shape[0]

    def total(role):
        value = windows[0][role * half : (role + 1) * half]
        for window in windows[1:]:
            value = value + window[role * half : (role + 1) * half]
        return value

    far_ref[...] = total(0)
    near_ref[...] = total(1)
    here_ref[...] = total(2) + own_ref[...]
    mate_ref[:half] = total(3)
    mate_ref[half:] = total(4)


def fetch(panel_hbm, panel_ref, sem):
    span = panel_ref.shape[1] // CHUNKS
    copies = []
    for chunk in range(CHUNKS):
        lanes = pl.ds(chunk * span, span)
        copies.append(pltpu.make_async_copy(panel_hbm.at[:, lanes], panel_ref.at[:, lanes], sem.at[chunk]))
    for copy in copies:
        copy.start()
    return copies


def panels(copies, panel_ref, count):
    per = count // 4 // CHUNKS

    def panel_of(quad):
        if quad % per == 0:
            copies[quad // per].wait()
        return panel_ref[:, quad * QUAD : (quad + 1) * QUAD]

    return panel_of


def first_kernel(cols_ref, place_ref, panel_hbm, start_ref, far_ref, near_ref, here_ref, mate_ref, panel_ref, vb_ref, own_ref, stage_ref, sem, *windows):
    copies = fetch(panel_hbm, panel_ref, sem)
    vb_ref[...] = start_ref[...].astype(jnp.bfloat16)
    panel_of = panels(copies, panel_ref, cols_ref.shape[1])
    scatter(vb_ref, panel_of, cols_ref, place_ref[0], windows, own_ref, stage_ref)
    hand_out(windows, own_ref, far_ref, near_ref, here_ref, mate_ref)


def residual_and_update(quad, right_ref, from_ref, inv_ref, parts):
    lanes = slice(quad * QUAD, (quad + 1) * QUAD)
    sums = []
    for pair in (2 * quad, 2 * quad + 1):
        total = parts[0][pair]
        for part in parts[1:]:
            total = total + part[pair]
        sums.append(total)
    res = right_ref[:, lanes] - jnp.concatenate(sums, 1)
    inv = inv_ref[:, lanes]
    weights = jnp.concatenate([masked_lanes(inv, e) for e in range(4)], 0)
    update = lax.dot_general(res.astype(jnp.bfloat16), weights, (((1,), (1,)), ((), ())), preferred_element_type=jnp.float32)
    return res, from_ref[:, lanes] + update


def second_kernel(cols_ref, place_ref, panel_hbm, right_ref, start_ref, inv_ref, here_in, mate_in, far_in, near_in,
                  first_ref, far_ref, near_ref, here_ref, mate_ref, panel_ref, vb_ref, own_ref, stage_ref, sem, *windows):
    copies = fetch(panel_hbm, panel_ref, sem)
    count = cols_ref.shape[1]
    for quad in range(count // 4):
        _, first = residual_and_update(quad, right_ref, start_ref, inv_ref, (here_in, mate_in, far_in, near_in))
        lanes = slice(quad * QUAD, (quad + 1) * QUAD)
        first_ref[:, lanes] = first
        vb_ref[:, lanes] = first.astype(jnp.bfloat16)
    panel_of = panels(copies, panel_ref, count)
    scatter(vb_ref, panel_of, cols_ref, place_ref[0], windows, own_ref, stage_ref)
    hand_out(windows, own_ref, far_ref, near_ref, here_ref, mate_ref)


def last_kernel(right_ref, first_ref, inv_ref, here_in, mate_in, far_in, near_in, adjoint_ref, residual_ref):
    for quad in range(right_ref.shape[1] // QUAD):
        lanes = slice(quad * QUAD, (quad + 1) * QUAD)
        res, adjoint = residual_and_update(quad, right_ref, first_ref, inv_ref, (here_in, mate_in, far_in, near_in))
        residual_ref[:, lanes] = res
        adjoint_ref[:, lanes] = adjoint


VMEM = pl.BlockSpec(memory_space=pltpu.VMEM)
SMEM = pl.BlockSpec(memory_space=pltpu.SMEM)
ANY = pl.BlockSpec(memory_space=pl.ANY)
PARAMS = pltpu.CompilerParams(vmem_limit_bytes=40 * 1024 * 1024)


def slabs(width, count):
    slab = jax.ShapeDtypeStruct((count // 2, width, 2 * DOF), jnp.float32)
    double = jax.ShapeDtypeStruct((count, width, 2 * DOF), jnp.float32)
    return [slab, slab, slab, double]


def scratch(width, count):
    return [
        pltpu.VMEM((SLOTS * DOF, count * DOF), jnp.bfloat16),
        pltpu.VMEM((width, count * DOF), jnp.bfloat16),
        pltpu.VMEM((count // 2, width, 2 * DOF), jnp.float32),
        pltpu.VMEM((2, 4 * width, 8 * DOF), jnp.float32),
        pltpu.SemaphoreType.DMA((CHUNKS,)),
    ] + [pltpu.VMEM((5 * count // 2, width, 2 * DOF), jnp.float32)] * WINDOWS


def exchange(far, near, mate):
    size = lax.axis_size("elem")
    half = near.shape[0]
    outward = [(i, i + 2) for i in range(1, size - 2, 2)] + [(i, i - 2) for i in range(2, size, 2)]
    across = [(i, i + 1) for i in range(1, size - 1, 2)] + [(i + 1, i) for i in range(1, size - 1, 2)]
    far = lax.ppermute(far, "elem", outward)
    mate = lax.ppermute(mate, "elem", [(i, i ^ 1) for i in range(size)])
    near = lax.ppermute(near + mate[half:], "elem", across)
    return far, near, mate[:half]


def body(blocks, cols, inverse, right_side, start):
    width = start.shape[0]
    count = cols.shape[1]
    panel = blocks.T
    place = lax.axis_index("elem").astype(jnp.int32).reshape(1)
    out = jax.ShapeDtypeStruct(start.shape, jnp.float32)
    far, near, here, mate = pl.pallas_call(
        first_kernel,
        out_shape=slabs(width, count),
        in_specs=[SMEM, SMEM, ANY, VMEM],
        out_specs=[VMEM] * 4,
        scratch_shapes=scratch(width, count),
        compiler_params=PARAMS,
    )(cols, place, panel, start)
    far, near, mate = exchange(far, near, mate)
    first, far, near, here, mate = pl.pallas_call(
        second_kernel,
        out_shape=[out] + slabs(width, count),
        in_specs=[SMEM, SMEM, ANY] + [VMEM] * 7,
        out_specs=[VMEM] * 5,
        scratch_shapes=scratch(width, count),
        compiler_params=PARAMS,
    )(cols, place, panel, right_side, start, inverse, here, mate, far, near)
    far, near, mate = exchange(far, near, mate)
    adjoint, residual = pl.pallas_call(
        last_kernel,
        out_shape=[out, out],
        in_specs=[VMEM] * 7,
        out_specs=[VMEM] * 2,
        compiler_params=PARAMS,
    )(right_side, first, inverse, here, mate, far, near)
    return (adjoint, residual)


def solution(mesh):
    return jax.shard_map(
        body,
        mesh=mesh,
        in_specs=(
            P("elem", None),
            P(None, "elem"),
            P(None, "elem"),
            P("rhs", "elem"),
            P("rhs", "elem"),
        ),
        out_specs=(P("rhs", "elem"), P("rhs", "elem")),
        check_vma=False,
    )
```

```python
import jax
import jax.numpy as jnp
from jax import lax
from jax.experimental import pallas as pl
from jax.experimental.pallas import tpu as pltpu
from jax.sharding import PartitionSpec as P

DOF = 64
SLOTS = 7
QUAD = 4 * DOF
CHUNKS = 8


def masked_lanes(value, part):
    lane = lax.broadcasted_iota(jnp.int32, value.shape, 1)
    return jnp.where(lane // DOF == part, value, jnp.zeros_like(value))


def products(vb, panel):
    spread = jnp.concatenate([masked_lanes(vb, e) for e in range(4)], 0)
    return lax.dot_general(spread, panel, (((1,), (1,)), ((), ())), preferred_element_type=jnp.float32)


def scatter(vb_ref, panel_of, cols_ref, device, window, own_ref, stage_ref):
    width = vb_ref.shape[0]
    count = cols_ref.shape[1]
    low = lax.broadcasted_iota(jnp.int32, (width, 2 * DOF), 1) < DOF
    base = (device - 2) * count
    for quad in range(count // 4):
        stage = stage_ref.at[quad]
        stage[:, : SLOTS * DOF] = products(vb_ref[:, quad * QUAD : (quad + 1) * QUAD], panel_of(quad))
        for e in range(4):
            rows = slice(e * width, (e + 1) * width)
            for s in range(1, SLOTS):
                tile = stage[rows, (s // 2) * 2 * DOF : (s // 2 + 1) * 2 * DOF]
                place = cols_ref[s - 1, 4 * quad + e] - base
                window[place] += jnp.where(low, tile, 0.0) if s % 2 == 0 else jnp.where(low, 0.0, tile)
        for pair in range(2):
            even = stage[2 * pair * width : (2 * pair + 1) * width, : 2 * DOF]
            odd = stage[(2 * pair + 1) * width : (2 * pair + 2) * width, : 2 * DOF]
            own_ref[2 * quad + pair] = jnp.where(low, even, pltpu.roll(odd, DOF, 1))


def hand_out(device, window, own_ref, far_ref, near_ref, here_ref, mate_ref):
    half, width, lanes = own_ref.shape
    low = lax.broadcasted_iota(jnp.int32, (width, lanes), 1) < DOF
    core = lax.rem(device, 2)

    def slab(role, out, at=0, more=None):
        first = (core * (4 - role) + (1 - core) * role) * 2 * half
        for pair in range(half):
            even = window[first + 2 * pair]
            odd = window[first + 2 * pair + 1]
            total = jnp.where(low, even, odd) + pltpu.roll(jnp.where(low, odd, even), DOF, 1)
            out[at + pair] = total if more is None else total + more[pair]

    slab(0, far_ref)
    slab(3, mate_ref)
    slab(4, mate_ref, half)
    slab(1, near_ref)
    slab(2, here_ref, 0, own_ref)


def fetch(panel_hbm, panel_ref, sem):
    span = panel_ref.shape[1] // CHUNKS
    copies = []
    for chunk in range(CHUNKS):
        lanes = pl.ds(chunk * span, span)
        copies.append(pltpu.make_async_copy(panel_hbm.at[:, lanes], panel_ref.at[:, lanes], sem.at[chunk]))
    for copy in copies:
        copy.start()
    return copies


def panels(copies, panel_ref, count):
    per = count // 4 // CHUNKS

    def panel_of(quad):
        if quad % per == 0:
            copies[quad // per].wait()
        return panel_ref[:, quad * QUAD : (quad + 1) * QUAD]

    return panel_of


def first_kernel(place_ref, cols_hbm, panel_hbm, start_hbm, far_ref, near_ref, here_ref, mate_ref,
                 cols_ref, start_ref, panel_ref, vb_ref, own_ref, stage_ref, window, sem):
    device = place_ref[0]
    small = pltpu.make_async_copy(cols_hbm, cols_ref, sem.at[CHUNKS])
    begin = pltpu.make_async_copy(start_hbm, start_ref, sem.at[CHUNKS + 1])
    begin.start()
    small.start()
    copies = fetch(panel_hbm, panel_ref, sem)
    window[...] = jnp.zeros_like(window)
    begin.wait()
    vb_ref[...] = start_ref[...].astype(jnp.bfloat16)
    small.wait()
    scatter(vb_ref, panels(copies, panel_ref, cols_ref.shape[1]), cols_ref, device, window, own_ref, stage_ref)
    hand_out(device, window, own_ref, far_ref, near_ref, here_ref, mate_ref)


def residual_and_update(quad, right_ref, from_ref, inv_ref, parts):
    lanes = slice(quad * QUAD, (quad + 1) * QUAD)
    sums = []
    for pair in (2 * quad, 2 * quad + 1):
        total = parts[0][pair]
        for part in parts[1:]:
            total = total + part[pair]
        sums.append(total)
    res = right_ref[:, lanes] - jnp.concatenate(sums, 1)
    inv = inv_ref[:, lanes]
    weights = jnp.concatenate([masked_lanes(inv, e) for e in range(4)], 0)
    update = lax.dot_general(res.astype(jnp.bfloat16), weights, (((1,), (1,)), ((), ())), preferred_element_type=jnp.float32)
    return res, from_ref[:, lanes] + update


def second_kernel(place_ref, cols_hbm, panel_hbm, right_ref, start_ref, inv_ref, here_in, mate_in, far_in, near_in,
                  first_ref, far_ref, near_ref, here_ref, mate_ref,
                  cols_ref, panel_ref, vb_ref, own_ref, stage_ref, window, sem):
    device = place_ref[0]
    count = cols_ref.shape[1]
    small = pltpu.make_async_copy(cols_hbm, cols_ref, sem.at[CHUNKS])
    small.start()
    copies = fetch(panel_hbm, panel_ref, sem)
    window[...] = jnp.zeros_like(window)
    for quad in range(count // 4):
        _, first = residual_and_update(quad, right_ref, start_ref, inv_ref, (here_in, mate_in, far_in, near_in))
        lanes = slice(quad * QUAD, (quad + 1) * QUAD)
        first_ref[:, lanes] = first
        vb_ref[:, lanes] = first.astype(jnp.bfloat16)
    small.wait()
    scatter(vb_ref, panels(copies, panel_ref, count), cols_ref, device, window, own_ref, stage_ref)
    hand_out(device, window, own_ref, far_ref, near_ref, here_ref, mate_ref)


def last_kernel(right_ref, first_ref, inv_ref, here_in, mate_in, far_in, near_in, adjoint_ref, residual_ref):
    for quad in range(right_ref.shape[1] // QUAD):
        lanes = slice(quad * QUAD, (quad + 1) * QUAD)
        res, adjoint = residual_and_update(quad, right_ref, first_ref, inv_ref, (here_in, mate_in, far_in, near_in))
        residual_ref[:, lanes] = res
        adjoint_ref[:, lanes] = adjoint


VMEM = pl.BlockSpec(memory_space=pltpu.VMEM)
SMEM = pl.BlockSpec(memory_space=pltpu.SMEM)
HBM = pl.BlockSpec(memory_space=pltpu.HBM)
PARAMS = pltpu.CompilerParams(vmem_limit_bytes=40 * 1024 * 1024)


def slabs(width, count):
    slab = jax.ShapeDtypeStruct((count // 2, width, 2 * DOF), jnp.float32)
    double = jax.ShapeDtypeStruct((count, width, 2 * DOF), jnp.float32)
    return [slab, slab, slab, double]


def scratch(width, count):
    return [
        pltpu.VMEM((SLOTS * DOF, count * DOF), jnp.bfloat16),
        pltpu.VMEM((width, count * DOF), jnp.bfloat16),
        pltpu.VMEM((count // 2, width, 2 * DOF), jnp.float32),
        pltpu.VMEM((count // 4, 4 * width, 8 * DOF), jnp.float32),
        pltpu.VMEM((5 * count, width, 2 * DOF), jnp.float32),
        pltpu.SemaphoreType.DMA((CHUNKS + 2,)),
    ]


def exchange(far, near, mate):
    size = lax.axis_size("elem")
    half = near.shape[0]
    outward = [(i, i + 2) for i in range(1, size - 2, 2)] + [(i, i - 2) for i in range(2, size, 2)]
    across = [(i, i + 1) for i in range(1, size - 1, 2)] + [(i + 1, i) for i in range(1, size - 1, 2)]
    far = lax.ppermute(far, "elem", outward)
    mate = lax.ppermute(mate, "elem", [(i, i ^ 1) for i in range(size)])
    near = lax.ppermute(near + mate[half:], "elem", across)
    return far, near, mate[:half]


def body(blocks, cols, inverse, right_side, start):
    width = start.shape[0]
    count = cols.shape[1]
    panel = blocks.T
    place = lax.axis_index("elem").astype(jnp.int32).reshape(1)
    out = jax.ShapeDtypeStruct(start.shape, jnp.float32)
    far, near, here, mate = pl.pallas_call(
        first_kernel,
        out_shape=slabs(width, count),
        in_specs=[SMEM, HBM, HBM, HBM],
        out_specs=[VMEM] * 4,
        scratch_shapes=[pltpu.SMEM(cols.shape, jnp.int32), pltpu.VMEM(start.shape, jnp.float32)] + scratch(width, count),
        compiler_params=PARAMS,
    )(place, cols, panel, start)
    far, near, mate = exchange(far, near, mate)
    first, far, near, here, mate = pl.pallas_call(
        second_kernel,
        out_shape=[out] + slabs(width, count),
        in_specs=[SMEM, HBM, HBM] + [VMEM] * 7,
        out_specs=[VMEM] * 5,
        scratch_shapes=[pltpu.SMEM(cols.shape, jnp.int32)] + scratch(width, count),
        compiler_params=PARAMS,
    )(place, cols, panel, right_side, start, inverse, here, mate, far, near)
    far, near, mate = exchange(far, near, mate)
    adjoint, residual = pl.pallas_call(
        last_kernel,
        out_shape=[out, out],
        in_specs=[VMEM] * 7,
        out_specs=[VMEM] * 2,
        compiler_params=PARAMS,
    )(right_side, first, inverse, here, mate, far, near)
    return (adjoint, residual)


def solution(mesh):
    return jax.shard_map(
        body,
        mesh=mesh,
        in_specs=(
            P("elem", None),
            P(None, "elem"),
            P(None, "elem"),
            P("rhs", "elem"),
            P("rhs", "elem"),
        ),
        out_specs=(P("rhs", "elem"), P("rhs", "elem")),
        check_vma=False,
    )
```

```python
import jax
import jax.numpy as jnp
from jax import lax
from jax.experimental import pallas as pl
from jax.experimental.pallas import tpu as pltpu
from jax.sharding import PartitionSpec as P

DOF = 64
SLOTS = 7
QUAD = 4 * DOF
CHUNKS = 8


def masked_lanes(value, part):
    lane = lax.broadcasted_iota(jnp.int32, value.shape, 1)
    return jnp.where(lane // DOF == part, value, jnp.zeros_like(value))


def products(vb, panel):
    spread = jnp.concatenate([masked_lanes(vb, e) for e in range(4)], 0)
    return lax.dot_general(spread, panel, (((1,), (1,)), ((), ())), preferred_element_type=jnp.float32)


def scatter(vb_ref, panel_of, cols_ref, device, window, own_ref, stage_ref):
    width = vb_ref.shape[0]
    count = cols_ref.shape[1]
    low = lax.broadcasted_iota(jnp.int32, (width, 2 * DOF), 1) < DOF
    base = (device - 2) * count
    for quad in range(count // 4):
        stage = stage_ref.at[quad]
        stage[:, : SLOTS * DOF] = products(vb_ref[:, quad * QUAD : (quad + 1) * QUAD], panel_of(quad))
        for e in range(4):
            rows = slice(e * width, (e + 1) * width)
            for s in range(1, SLOTS):
                tile = stage[rows, (s // 2) * 2 * DOF : (s // 2 + 1) * 2 * DOF]
                place = cols_ref[s - 1, 4 * quad + e] - base
                window[place] += jnp.where(low, tile, 0.0) if s % 2 == 0 else jnp.where(low, 0.0, tile)
        for pair in range(2):
            even = stage[2 * pair * width : (2 * pair + 1) * width, : 2 * DOF]
            odd = stage[(2 * pair + 1) * width : (2 * pair + 2) * width, : 2 * DOF]
            own_ref[2 * quad + pair] = jnp.where(low, even, pltpu.roll(odd, DOF, 1))


def hand_out(device, window, role, out, at=0, more=None):
    half = window.shape[0] // 10
    low = lax.broadcasted_iota(jnp.int32, window.shape[1:], 1) < DOF
    core = lax.rem(device, 2)
    first = (core * (4 - role) + (1 - core) * role) * 2 * half
    for pair in range(half):
        even = window[first + 2 * pair]
        odd = window[first + 2 * pair + 1]
        total = jnp.where(low, even, odd) + pltpu.roll(jnp.where(low, odd, even), DOF, 1)
        out[at + pair] = total if more is None else total + more[pair]


def mate_kernel(place_ref, window, mate_ref):
    half = mate_ref.shape[0] // 2
    hand_out(place_ref[0], window, 3, mate_ref)
    hand_out(place_ref[0], window, 4, mate_ref, half)


def rest_kernel(place_ref, window, own_ref, near_ref, here_ref):
    hand_out(place_ref[0], window, 1, near_ref)
    hand_out(place_ref[0], window, 2, here_ref, 0, own_ref)


def fetch(panel_hbm, panel_ref, sem):
    span = panel_ref.shape[1] // CHUNKS
    copies = []
    for chunk in range(CHUNKS):
        lanes = pl.ds(chunk * span, span)
        copies.append(pltpu.make_async_copy(panel_hbm.at[:, lanes], panel_ref.at[:, lanes], sem.at[chunk]))
    for copy in copies:
        copy.start()
    return copies


def panels(copies, panel_ref, count):
    per = count // 4 // CHUNKS

    def panel_of(quad):
        if copies and quad % per == 0:
            copies[quad // per].wait()
        return panel_ref[:, quad * QUAD : (quad + 1) * QUAD]

    return panel_of


def first_kernel(place_ref, cols_hbm, panel_hbm, start_hbm, far_ref, window, own_ref, panel_ref,
                 cols_ref, start_ref, vb_ref, stage_ref, sem):
    device = place_ref[0]
    small = pltpu.make_async_copy(cols_hbm, cols_ref, sem.at[CHUNKS])
    begin = pltpu.make_async_copy(start_hbm, start_ref, sem.at[CHUNKS + 1])
    begin.start()
    small.start()
    copies = fetch(panel_hbm, panel_ref, sem)
    window[...] = jnp.zeros_like(window)
    begin.wait()
    vb_ref[...] = start_ref[...].astype(jnp.bfloat16)
    small.wait()
    scatter(vb_ref, panels(copies, panel_ref, cols_ref.shape[1]), cols_ref, device, window, own_ref, stage_ref)
    hand_out(device, window, 0, far_ref)


def residual_and_update(quad, right_ref, from_ref, inv_ref, parts):
    lanes = slice(quad * QUAD, (quad + 1) * QUAD)
    sums = []
    for pair in (2 * quad, 2 * quad + 1):
        total = parts[0][pair]
        for part in parts[1:]:
            total = total + part[pair]
        sums.append(total)
    res = right_ref[:, lanes] - jnp.concatenate(sums, 1)
    inv = inv_ref[:, lanes]
    weights = jnp.concatenate([masked_lanes(inv, e) for e in range(4)], 0)
    update = lax.dot_general(res.astype(jnp.bfloat16), weights, (((1,), (1,)), ((), ())), preferred_element_type=jnp.float32)
    return res, from_ref[:, lanes] + update


def second_kernel(place_ref, cols_hbm, panel_ref, right_ref, start_ref, inv_ref, here_in, mate_in, far_in, near_in,
                  first_ref, far_ref, window, own_ref, cols_ref, vb_ref, stage_ref, sem):
    device = place_ref[0]
    count = cols_ref.shape[1]
    small = pltpu.make_async_copy(cols_hbm, cols_ref, sem.at[CHUNKS])
    small.start()
    window[...] = jnp.zeros_like(window)
    for quad in range(count // 4):
        _, first = residual_and_update(quad, right_ref, start_ref, inv_ref, (here_in, mate_in, far_in, near_in))
        lanes = slice(quad * QUAD, (quad + 1) * QUAD)
        first_ref[:, lanes] = first
        vb_ref[:, lanes] = first.astype(jnp.bfloat16)
    small.wait()
    scatter(vb_ref, panels((), panel_ref, count), cols_ref, device, window, own_ref, stage_ref)
    hand_out(device, window, 0, far_ref)


def last_kernel(right_ref, first_ref, inv_ref, here_in, mate_in, far_in, near_in, adjoint_ref, residual_ref):
    for quad in range(right_ref.shape[1] // QUAD):
        lanes = slice(quad * QUAD, (quad + 1) * QUAD)
        res, adjoint = residual_and_update(quad, right_ref, first_ref, inv_ref, (here_in, mate_in, far_in, near_in))
        residual_ref[:, lanes] = res
        adjoint_ref[:, lanes] = adjoint


VMEM = pl.BlockSpec(memory_space=pltpu.VMEM)
SMEM = pl.BlockSpec(memory_space=pltpu.SMEM)
HBM = pl.BlockSpec(memory_space=pltpu.HBM)
PARAMS = pltpu.CompilerParams(vmem_limit_bytes=40 * 1024 * 1024)


def applied(width, count):
    slab = jax.ShapeDtypeStruct((count // 2, width, 2 * DOF), jnp.float32)
    window = jax.ShapeDtypeStruct((5 * count, width, 2 * DOF), jnp.float32)
    return [slab, window, slab]


def scratch(width, count):
    return [
        pltpu.VMEM((width, count * DOF), jnp.bfloat16),
        pltpu.VMEM((count // 4, 4 * width, 8 * DOF), jnp.float32),
        pltpu.SemaphoreType.DMA((CHUNKS + 2,)),
    ]


def in_hbm(value):
    return pltpu.with_memory_space_constraint(value, pltpu.HBM)


def exchange(place, far, window, own):
    size = lax.axis_size("elem")
    half, width, lanes = own.shape
    slab = jax.ShapeDtypeStruct(own.shape, jnp.float32)
    double = jax.ShapeDtypeStruct((2 * half, width, lanes), jnp.float32)
    outward = [(i, i + 2) for i in range(1, size - 2, 2)] + [(i, i - 2) for i in range(2, size, 2)]
    across = [(i, i + 1) for i in range(1, size - 1, 2)] + [(i + 1, i) for i in range(1, size - 1, 2)]
    far = lax.ppermute(far, "elem", outward)
    mate = pl.pallas_call(
        mate_kernel,
        out_shape=double,
        in_specs=[SMEM, VMEM],
        out_specs=VMEM,
        compiler_params=PARAMS,
        cost_estimate=pl.CostEstimate(flops=10**8, bytes_accessed=4 * 10**6, transcendentals=0),
    )(place, window)
    mate = lax.ppermute(mate, "elem", [(i, i ^ 1) for i in range(size)])
    near, here = pl.pallas_call(
        rest_kernel,
        out_shape=[slab, slab],
        in_specs=[SMEM, VMEM, VMEM],
        out_specs=[VMEM, VMEM],
        compiler_params=PARAMS,
        cost_estimate=pl.CostEstimate(flops=10**10, bytes_accessed=4 * 10**6, transcendentals=0),
    )(place, window, own)
    near = lax.ppermute(near + mate[half:], "elem", across)
    return here, mate[:half], far, near


def body(blocks, cols, inverse, right_side, start):
    width = start.shape[0]
    count = cols.shape[1]
    place = lax.axis_index("elem").astype(jnp.int32).reshape(1)
    out = jax.ShapeDtypeStruct(start.shape, jnp.float32)
    cols = in_hbm(cols)
    far, window, own, panel = pl.pallas_call(
        first_kernel,
        out_shape=applied(width, count) + [pltpu.VMEM(blocks.shape[::-1], jnp.bfloat16)],
        in_specs=[SMEM, HBM, HBM, HBM],
        out_specs=[VMEM] * 4,
        scratch_shapes=[pltpu.SMEM(cols.shape, jnp.int32), pltpu.VMEM(start.shape, jnp.float32)] + scratch(width, count),
        compiler_params=PARAMS,
    )(place, cols, in_hbm(blocks.T), in_hbm(start))
    parts = exchange(place, far, window, own)
    first, far, window, own = pl.pallas_call(
        second_kernel,
        out_shape=[out] + applied(width, count),
        in_specs=[SMEM, HBM] + [VMEM] * 8,
        out_specs=[VMEM] * 4,
        scratch_shapes=[pltpu.SMEM(cols.shape, jnp.int32)] + scratch(width, count),
        compiler_params=PARAMS,
    )(place, cols, panel, right_side, start, inverse, *parts)
    parts = exchange(place, far, window, own)
    adjoint, residual = pl.pallas_call(
        last_kernel,
        out_shape=[out, out],
        in_specs=[VMEM] * 7,
        out_specs=[VMEM] * 2,
        compiler_params=PARAMS,
    )(right_side, first, inverse, *parts)
    return (adjoint, residual)


def solution(mesh):
    return jax.shard_map(
        body,
        mesh=mesh,
        in_specs=(
            P("elem", None),
            P(None, "elem"),
            P(None, "elem"),
            P("rhs", "elem"),
            P("rhs", "elem"),
        ),
        out_specs=(P("rhs", "elem"), P("rhs", "elem")),
        check_vma=False,
    )
```

```python
import jax
import jax.numpy as jnp
from jax import lax
from jax.experimental import pallas as pl
from jax.experimental.pallas import tpu as pltpu
from jax.sharding import PartitionSpec as P

DOF = 64
SLOTS = 7
QUAD = 4 * DOF
CHUNKS = 4
WINDOWS = 2
PIECES = 2


def masked_lanes(value, part):
    lane = lax.broadcasted_iota(jnp.int32, value.shape, 1)
    return jnp.where(lane // DOF == part, value, jnp.zeros_like(value))


def products(vb, panel):
    spread = jnp.concatenate([masked_lanes(vb, e) for e in range(4)], 0)
    return lax.dot_general(spread, panel, (((1,), (1,)), ((), ())), preferred_element_type=jnp.float32)


def scatter(vb_ref, panel_of, cols_ref, device, windows, own_ref, stage_ref):
    width = vb_ref.shape[0]
    count = cols_ref.shape[1]
    low = lax.broadcasted_iota(jnp.int32, (width, 2 * DOF), 1) < DOF
    base = (device - 2) * count
    for quad in range(count // 4):
        stage = stage_ref.at[quad]
        stage[:, : SLOTS * DOF] = products(vb_ref[:, quad * QUAD : (quad + 1) * QUAD], panel_of(quad))
        for e in range(4):
            rows = slice(e * width, (e + 1) * width)
            for s in range(1, SLOTS):
                tile = stage[rows, (s // 2) * 2 * DOF : (s // 2 + 1) * 2 * DOF]
                place = cols_ref[s - 1, 4 * quad + e] - base
                windows[s % WINDOWS][place] += jnp.where(low, tile, 0.0) if s % 2 == 0 else jnp.where(low, 0.0, tile)
        for pair in range(2):
            even = stage[2 * pair * width : (2 * pair + 1) * width, : 2 * DOF]
            odd = stage[(2 * pair + 1) * width : (2 * pair + 2) * width, : 2 * DOF]
            own_ref[2 * quad + pair] = jnp.where(low, even, pltpu.roll(odd, DOF, 1))


def sum_of(windows, place):
    total = windows[0][place]
    for window in windows[1:]:
        total = total + window[place]
    return total


def clear(windows):
    for window in windows:
        window[...] = jnp.zeros_like(window)


def hand_out(device, windows, role, out, at=0, more=None):
    half = windows[0].shape[0] // 10
    low = lax.broadcasted_iota(jnp.int32, windows[0].shape[1:], 1) < DOF
    core = lax.rem(device, 2)
    first = (core * (4 - role) + (1 - core) * role) * 2 * half
    for pair in range(half):
        even = sum_of(windows, first + 2 * pair)
        odd = sum_of(windows, first + 2 * pair + 1)
        total = jnp.where(low, even, odd) + pltpu.roll(jnp.where(low, odd, even), DOF, 1)
        out[at + pair] = total if more is None else total + more[pair]


def mate_kernel(place_ref, *refs):
    windows, (mate_ref,) = refs[:WINDOWS], refs[WINDOWS:]
    half = mate_ref.shape[0] // 2
    hand_out(place_ref[0], windows, 3, mate_ref)
    hand_out(place_ref[0], windows, 4, mate_ref, half)


def rest_kernel(place_ref, *refs):
    windows, (own_ref, near_ref, here_ref) = refs[:WINDOWS], refs[WINDOWS:]
    hand_out(place_ref[0], windows, 1, near_ref)
    hand_out(place_ref[0], windows, 2, here_ref, 0, own_ref)


def fetch(panel_hbm, panel_ref, sem):
    span = panel_ref.shape[1] // CHUNKS
    copies = []
    for chunk in range(CHUNKS):
        lanes = pl.ds(chunk * span, span)
        copies.append(pltpu.make_async_copy(panel_hbm.at[:, lanes], panel_ref.at[:, lanes], sem.at[chunk]))
    for copy in copies:
        copy.start()
    return copies


def panels(copies, panel_ref, count):
    per = count // 4 // CHUNKS

    def panel_of(quad):
        if copies and quad % per == 0:
            copies[quad // per].wait()
        return panel_ref[:, quad * QUAD : (quad + 1) * QUAD]

    return panel_of


def first_kernel(place_ref, cols_hbm, panel_hbm, start_hbm, *refs):
    windows, (own_ref, far_ref, panel_ref, cols_ref, start_ref, vb_ref, stage_ref, sem) = refs[:WINDOWS], refs[WINDOWS:]
    device = place_ref[0]
    small = pltpu.make_async_copy(cols_hbm, cols_ref, sem.at[CHUNKS])
    begin = pltpu.make_async_copy(start_hbm, start_ref, sem.at[CHUNKS + 1])
    begin.start()
    small.start()
    copies = fetch(panel_hbm, panel_ref, sem)
    clear(windows)
    begin.wait()
    vb_ref[...] = start_ref[...].astype(jnp.bfloat16)
    small.wait()
    scatter(vb_ref, panels(copies, panel_ref, cols_ref.shape[1]), cols_ref, device, windows, own_ref, stage_ref)
    hand_out(device, windows, 0, far_ref)


def residual_and_update(quad, right_ref, from_ref, inv_ref, parts):
    lanes = slice(quad * QUAD, (quad + 1) * QUAD)
    sums = []
    for pair in (2 * quad, 2 * quad + 1):
        total = parts[0][pair]
        for part in parts[1:]:
            total = total + part[pair]
        sums.append(total)
    res = right_ref[:, lanes] - jnp.concatenate(sums, 1)
    inv = inv_ref[:, lanes]
    weights = jnp.concatenate([masked_lanes(inv, e) for e in range(4)], 0)
    update = lax.dot_general(res.astype(jnp.bfloat16), weights, (((1,), (1,)), ((), ())), preferred_element_type=jnp.float32)
    return res, from_ref[:, lanes] + update


def second_kernel(place_ref, cols_hbm, panel_ref, right_ref, start_ref, inv_ref, here_in, mate_in, far_in, near_in, *refs):
    windows, (own_ref, far_ref, first_ref, cols_ref, vb_ref, stage_ref, sem) = refs[:WINDOWS], refs[WINDOWS:]
    device = place_ref[0]
    count = cols_ref.shape[1]
    small = pltpu.make_async_copy(cols_hbm, cols_ref, sem.at[CHUNKS])
    small.start()
    clear(windows)
    for quad in range(count // 4):
        _, first = residual_and_update(quad, right_ref, start_ref, inv_ref, (here_in, mate_in, far_in, near_in))
        lanes = slice(quad * QUAD, (quad + 1) * QUAD)
        first_ref[:, lanes] = first
        vb_ref[:, lanes] = first.astype(jnp.bfloat16)
    small.wait()
    scatter(vb_ref, panels((), panel_ref, count), cols_ref, device, windows, own_ref, stage_ref)
    hand_out(device, windows, 0, far_ref)


def last_kernel(right_ref, first_ref, inv_ref, here_in, mate_in, far_in, near_in, adjoint_hbm, residual_hbm, adjoint_ref, residual_ref, sem):
    quads = right_ref.shape[1] // QUAD
    copies = []
    for quad in range(quads):
        lanes = slice(quad * QUAD, (quad + 1) * QUAD)
        res, adjoint = residual_and_update(quad, right_ref, first_ref, inv_ref, (here_in, mate_in, far_in, near_in))
        residual_ref[:, lanes] = res
        adjoint_ref[:, lanes] = adjoint
        if (quad + 1) % (quads // PIECES) == 0:
            piece = quad // (quads // PIECES)
            done = pl.ds(piece * (quads // PIECES) * QUAD, quads // PIECES * QUAD)
            for i, (kept, out) in enumerate(((residual_ref, residual_hbm), (adjoint_ref, adjoint_hbm))):
                copies.append(pltpu.make_async_copy(kept.at[:, done], out.at[:, done], sem.at[i, piece]))
                copies[-1].start()
    for copy in copies:
        copy.wait()


VMEM = pl.BlockSpec(memory_space=pltpu.VMEM)
SMEM = pl.BlockSpec(memory_space=pltpu.SMEM)
HBM = pl.BlockSpec(memory_space=pltpu.HBM)
PARAMS = pltpu.CompilerParams(vmem_limit_bytes=40 * 1024 * 1024)


def applied(width, count):
    slab = jax.ShapeDtypeStruct((count // 2, width, 2 * DOF), jnp.float32)
    window = jax.ShapeDtypeStruct((5 * count, width, 2 * DOF), jnp.float32)
    return [window] * WINDOWS + [slab, slab]


def scratch(width, count):
    return [
        pltpu.VMEM((width, count * DOF), jnp.bfloat16),
        pltpu.VMEM((count // 4, 4 * width, 8 * DOF), jnp.float32),
        pltpu.SemaphoreType.DMA((CHUNKS + 2,)),
    ]


def in_hbm(value):
    return pltpu.with_memory_space_constraint(value, pltpu.HBM)


def exchange(place, windows, own, far):
    size = lax.axis_size("elem")
    half, width, lanes = own.shape
    slab = jax.ShapeDtypeStruct(own.shape, jnp.float32)
    double = jax.ShapeDtypeStruct((2 * half, width, lanes), jnp.float32)
    outward = [(i, i + 2) for i in range(1, size - 2, 2)] + [(i, i - 2) for i in range(2, size, 2)]
    across = [(i, i + 1) for i in range(1, size - 1, 2)] + [(i + 1, i) for i in range(1, size - 1, 2)]
    far = lax.ppermute(far, "elem", outward)
    mate = pl.pallas_call(
        mate_kernel,
        out_shape=double,
        in_specs=[SMEM] + [VMEM] * WINDOWS,
        out_specs=VMEM,
        compiler_params=PARAMS,
        cost_estimate=pl.CostEstimate(flops=10**8, bytes_accessed=4 * 10**6, transcendentals=0),
    )(place, *windows)
    mate = lax.ppermute(mate, "elem", [(i, i ^ 1) for i in range(size)])
    near, here = pl.pallas_call(
        rest_kernel,
        out_shape=[slab, slab],
        in_specs=[SMEM] + [VMEM] * (WINDOWS + 1),
        out_specs=[VMEM, VMEM],
        compiler_params=PARAMS,
        cost_estimate=pl.CostEstimate(flops=10**10, bytes_accessed=4 * 10**6, transcendentals=0),
    )(place, *windows, own)
    near = lax.ppermute(near + mate[half:], "elem", across)
    return here, mate[:half], far, near


def body(blocks, cols, inverse, right_side, start):
    width = start.shape[0]
    count = cols.shape[1]
    place = lax.axis_index("elem").astype(jnp.int32).reshape(1)
    out = jax.ShapeDtypeStruct(start.shape, jnp.float32)
    cols = in_hbm(cols)
    *windows, own, far, panel = pl.pallas_call(
        first_kernel,
        out_shape=applied(width, count) + [pltpu.VMEM(blocks.shape[::-1], jnp.bfloat16)],
        in_specs=[SMEM, HBM, HBM, HBM],
        out_specs=[VMEM] * (WINDOWS + 3),
        scratch_shapes=[pltpu.SMEM(cols.shape, jnp.int32), pltpu.VMEM(start.shape, jnp.float32)] + scratch(width, count),
        compiler_params=PARAMS,
    )(place, cols, in_hbm(blocks.T), in_hbm(start))
    parts = exchange(place, windows, own, far)
    *windows, own, far, first = pl.pallas_call(
        second_kernel,
        out_shape=applied(width, count) + [out],
        in_specs=[SMEM, HBM] + [VMEM] * 8,
        out_specs=[VMEM] * (WINDOWS + 3),
        scratch_shapes=[pltpu.SMEM(cols.shape, jnp.int32)] + scratch(width, count),
        compiler_params=PARAMS,
    )(place, cols, panel, right_side, start, inverse, *parts)
    parts = exchange(place, windows, own, far)
    adjoint, residual = pl.pallas_call(
        last_kernel,
        out_shape=[out, out],
        in_specs=[VMEM] * 7,
        out_specs=[HBM] * 2,
        scratch_shapes=[pltpu.VMEM(start.shape, jnp.float32)] * 2 + [pltpu.SemaphoreType.DMA((2, PIECES))],
        compiler_params=PARAMS,
    )(right_side, first, inverse, *parts)
    return (adjoint, residual)


def solution(mesh):
    return jax.shard_map(
        body,
        mesh=mesh,
        in_specs=(
            P("elem", None),
            P(None, "elem"),
            P(None, "elem"),
            P("rhs", "elem"),
            P("rhs", "elem"),
        ),
        out_specs=(P("rhs", "elem"), P("rhs", "elem")),
        check_vma=False,
    )
```

```python
import jax
import jax.numpy as jnp
from jax import lax
from jax.experimental import pallas as pl
from jax.experimental.pallas import tpu as pltpu
from jax.sharding import PartitionSpec as P

DOF = 64
SLOTS = 7
QUAD = 4 * DOF
CHUNKS = 2
WINDOWS = 2
PIECES = 2


def masked_lanes(value, part):
    lane = lax.broadcasted_iota(jnp.int32, value.shape, 1)
    return jnp.where(lane // DOF == part, value, jnp.zeros_like(value))


def products(vb, panel):
    spread = jnp.concatenate([masked_lanes(vb, e) for e in range(4)], 0)
    return lax.dot_general(spread, panel, (((1,), (1,)), ((), ())), preferred_element_type=jnp.float32)


def scatter(vb_ref, panel_of, cols_ref, device, windows, own_ref, stage_ref):
    width = vb_ref.shape[0]
    count = cols_ref.shape[1]
    low = lax.broadcasted_iota(jnp.int32, (width, 2 * DOF), 1) < DOF
    base = (device - 2) * count

    def multiply(quad):
        stage_ref[quad, :, : SLOTS * DOF] = products(vb_ref[:, quad * QUAD : (quad + 1) * QUAD], panel_of(quad))

    def add(quad):
        stage = stage_ref.at[quad]
        kept = None
        for e in range(4):
            rows = slice(e * width, (e + 1) * width)
            for pair in range(4):
                tile = stage[rows, pair * 2 * DOF : (pair + 1) * 2 * DOF]
                if pair == 0:
                    if e % 2 == 0:
                        kept = tile
                    else:
                        own_ref[2 * quad + e // 2] = jnp.where(low, kept, pltpu.roll(tile, DOF, 1))
                else:
                    place = cols_ref[2 * pair - 1, 4 * quad + e] - base
                    windows[0][place] += jnp.where(low, tile, 0.0)
                if pair < 3:
                    place = cols_ref[2 * pair, 4 * quad + e] - base
                    windows[1][place] += jnp.where(low, 0.0, tile)

    for quad in range(count // 4):
        multiply(quad)
        add(quad)


def sum_of(windows, place):
    total = windows[0][place]
    for window in windows[1:]:
        total = total + window[place]
    return total


def clear(windows):
    for window in windows:
        window[...] = jnp.zeros_like(window)


def hand_out(device, windows, role, out, at=0, more=None):
    half = windows[0].shape[0] // 10
    low = lax.broadcasted_iota(jnp.int32, windows[0].shape[1:], 1) < DOF
    core = lax.rem(device, 2)
    first = (core * (4 - role) + (1 - core) * role) * 2 * half
    for pair in range(half):
        even = sum_of(windows, first + 2 * pair)
        odd = sum_of(windows, first + 2 * pair + 1)
        total = jnp.where(low, even, odd) + pltpu.roll(jnp.where(low, odd, even), DOF, 1)
        out[at + pair] = total if more is None else total + more[pair]


def mate_kernel(place_ref, *refs):
    windows, (mate_ref,) = refs[:WINDOWS], refs[WINDOWS:]
    half = mate_ref.shape[0] // 2
    hand_out(place_ref[0], windows, 3, mate_ref)
    hand_out(place_ref[0], windows, 4, mate_ref, half)


def rest_kernel(place_ref, *refs):
    windows, (own_ref, near_ref, here_ref) = refs[:WINDOWS], refs[WINDOWS:]
    hand_out(place_ref[0], windows, 1, near_ref)
    hand_out(place_ref[0], windows, 2, here_ref, 0, own_ref)


def fetch(panel_hbm, panel_ref, sem):
    span = panel_ref.shape[1] // CHUNKS
    copies = []
    for chunk in range(CHUNKS):
        lanes = pl.ds(chunk * span, span)
        copies.append(pltpu.make_async_copy(panel_hbm.at[:, lanes], panel_ref.at[:, lanes], sem.at[chunk]))
    for copy in copies:
        copy.start()
    return copies


def panels(copies, panel_ref, count):
    per = count // 4 // CHUNKS

    def panel_of(quad):
        if copies and quad % per == 0:
            copies[quad // per].wait()
        return panel_ref[:, quad * QUAD : (quad + 1) * QUAD]

    return panel_of


def first_kernel(place_ref, cols_hbm, panel_hbm, start_hbm, *refs):
    windows, (own_ref, far_ref, panel_ref, cols_ref, start_ref, vb_ref, stage_ref, sem) = refs[:WINDOWS], refs[WINDOWS:]
    device = place_ref[0]
    small = pltpu.make_async_copy(cols_hbm, cols_ref, sem.at[CHUNKS])
    begin = pltpu.make_async_copy(start_hbm, start_ref, sem.at[CHUNKS + 1])
    begin.start()
    small.start()
    copies = fetch(panel_hbm, panel_ref, sem)
    clear(windows)
    begin.wait()
    vb_ref[...] = start_ref[...].astype(jnp.bfloat16)
    small.wait()
    scatter(vb_ref, panels(copies, panel_ref, cols_ref.shape[1]), cols_ref, device, windows, own_ref, stage_ref)
    hand_out(device, windows, 0, far_ref)


def residual_and_update(quad, right_ref, from_ref, inv_ref, parts):
    lanes = slice(quad * QUAD, (quad + 1) * QUAD)
    sums = []
    for pair in (2 * quad, 2 * quad + 1):
        total = parts[0][pair]
        for part in parts[1:]:
            total = total + part[pair]
        sums.append(total)
    res = right_ref[:, lanes] - jnp.concatenate(sums, 1)
    resb = res.astype(jnp.bfloat16)
    spread = jnp.concatenate([masked_lanes(resb, e) for e in range(4)], 0)
    out = lax.dot_general(spread, inv_ref[:, lanes], (((1,), (1,)), ((), ())), preferred_element_type=jnp.float32)
    width = res.shape[0]
    nothing = jnp.zeros((width, DOF), jnp.float32)
    each = [jnp.concatenate([out[e * width : (e + 1) * width], nothing], 1) for e in range(4)]
    update = jnp.concatenate([each[0] + pltpu.roll(each[1], DOF, 1), each[2] + pltpu.roll(each[3], DOF, 1)], 1)
    return res, from_ref[:, lanes] + update


def second_kernel(place_ref, cols_hbm, panel_ref, right_ref, start_ref, inv_ref, here_in, mate_in, far_in, near_in, *refs):
    windows, (own_ref, far_ref, first_ref, cols_ref, vb_ref, stage_ref, sem) = refs[:WINDOWS], refs[WINDOWS:]
    device = place_ref[0]
    count = cols_ref.shape[1]
    small = pltpu.make_async_copy(cols_hbm, cols_ref, sem.at[CHUNKS])
    small.start()
    clear(windows)
    for quad in range(count // 4):
        _, first = residual_and_update(quad, right_ref, start_ref, inv_ref, (here_in, mate_in, far_in, near_in))
        lanes = slice(quad * QUAD, (quad + 1) * QUAD)
        first_ref[:, lanes] = first
        vb_ref[:, lanes] = first.astype(jnp.bfloat16)
    small.wait()
    scatter(vb_ref, panels((), panel_ref, count), cols_ref, device, windows, own_ref, stage_ref)
    hand_out(device, windows, 0, far_ref)


def last_kernel(right_ref, first_ref, inv_ref, here_in, mate_in, far_in, near_in, adjoint_hbm, residual_hbm, adjoint_ref, residual_ref, sem):
    quads = right_ref.shape[1] // QUAD
    copies = []
    for quad in range(quads):
        lanes = slice(quad * QUAD, (quad + 1) * QUAD)
        res, adjoint = residual_and_update(quad, right_ref, first_ref, inv_ref, (here_in, mate_in, far_in, near_in))
        residual_ref[:, lanes] = res
        adjoint_ref[:, lanes] = adjoint
        if (quad + 1) % (quads // PIECES) == 0:
            piece = quad // (quads // PIECES)
            done = pl.ds(piece * (quads // PIECES) * QUAD, quads // PIECES * QUAD)
            for i, (kept, out) in enumerate(((residual_ref, residual_hbm), (adjoint_ref, adjoint_hbm))):
                copies.append(pltpu.make_async_copy(kept.at[:, done], out.at[:, done], sem.at[i, piece]))
                copies[-1].start()
    for copy in copies:
        copy.wait()


VMEM = pl.BlockSpec(memory_space=pltpu.VMEM)
SMEM = pl.BlockSpec(memory_space=pltpu.SMEM)
HBM = pl.BlockSpec(memory_space=pltpu.HBM)
PARAMS = pltpu.CompilerParams(vmem_limit_bytes=40 * 1024 * 1024)


def applied(width, count):
    slab = jax.ShapeDtypeStruct((count // 2, width, 2 * DOF), jnp.float32)
    window = jax.ShapeDtypeStruct((5 * count, width, 2 * DOF), jnp.float32)
    return [window] * WINDOWS + [slab, slab]


def scratch(width, count):
    return [
        pltpu.VMEM((width, count * DOF), jnp.bfloat16),
        pltpu.VMEM((count // 4, 4 * width, 8 * DOF), jnp.float32),
        pltpu.SemaphoreType.DMA((CHUNKS + 2,)),
    ]


def in_hbm(value):
    return pltpu.with_memory_space_constraint(value, pltpu.HBM)


def exchange(place, windows, own, far, hint):
    size = lax.axis_size("elem")
    half, width, lanes = own.shape
    slab = jax.ShapeDtypeStruct(own.shape, jnp.float32)
    double = jax.ShapeDtypeStruct((2 * half, width, lanes), jnp.float32)
    outward = [(i, i + 2) for i in range(1, size - 2, 2)] + [(i, i - 2) for i in range(2, size, 2)]
    across = [(i, i + 1) for i in range(1, size - 1, 2)] + [(i + 1, i) for i in range(1, size - 1, 2)]
    far = lax.ppermute(far, "elem", outward)
    mate = pl.pallas_call(
        mate_kernel,
        out_shape=double,
        in_specs=[SMEM] + [VMEM] * WINDOWS,
        out_specs=VMEM,
        compiler_params=PARAMS,
        cost_estimate=pl.CostEstimate(flops=10**8, bytes_accessed=4 * 10**6, transcendentals=0),
    )(place, *windows)
    mate = lax.ppermute(mate, "elem", [(i, i ^ 1) for i in range(size)])
    near, here = pl.pallas_call(
        rest_kernel,
        out_shape=[slab, slab],
        in_specs=[SMEM] + [VMEM] * (WINDOWS + 1),
        out_specs=[VMEM, VMEM],
        compiler_params=PARAMS,
        cost_estimate=pl.CostEstimate(flops=hint, bytes_accessed=4 * 10**6, transcendentals=0),
    )(place, *windows, own)
    near = lax.ppermute(near + mate[half:], "elem", across)
    return here, mate[:half], far, near


def body(blocks, cols, inverse, right_side, start):
    width = start.shape[0]
    count = cols.shape[1]
    place = lax.axis_index("elem").astype(jnp.int32).reshape(1)
    out = jax.ShapeDtypeStruct(start.shape, jnp.float32)
    cols = in_hbm(cols)
    *windows, own, far, panel = pl.pallas_call(
        first_kernel,
        out_shape=applied(width, count) + [pltpu.VMEM(blocks.shape[::-1], jnp.bfloat16)],
        in_specs=[SMEM, HBM, HBM, HBM],
        out_specs=[VMEM] * (WINDOWS + 3),
        scratch_shapes=[pltpu.SMEM(cols.shape, jnp.int32), pltpu.VMEM(start.shape, jnp.float32)] + scratch(width, count),
        compiler_params=PARAMS,
    )(place, cols, in_hbm(blocks.T), in_hbm(start))
    parts = exchange(place, windows, own, far, 10**8)
    *windows, own, far, first = pl.pallas_call(
        second_kernel,
        out_shape=applied(width, count) + [out],
        in_specs=[SMEM, HBM] + [VMEM] * 8,
        out_specs=[VMEM] * (WINDOWS + 3),
        scratch_shapes=[pltpu.SMEM(cols.shape, jnp.int32)] + scratch(width, count),
        compiler_params=PARAMS,
    )(place, cols, panel, right_side, start, inverse, *parts)
    parts = exchange(place, windows, own, far, 10**10)
    adjoint, residual = pl.pallas_call(
        last_kernel,
        out_shape=[out, out],
        in_specs=[VMEM] * 7,
        out_specs=[HBM] * 2,
        scratch_shapes=[pltpu.VMEM(start.shape, jnp.float32)] * 2 + [pltpu.SemaphoreType.DMA((2, PIECES))],
        compiler_params=PARAMS,
    )(right_side, first, inverse, *parts)
    return (adjoint, residual)


def solution(mesh):
    return jax.shard_map(
        body,
        mesh=mesh,
        in_specs=(
            P("elem", None),
            P(None, "elem"),
            P(None, "elem"),
            P("rhs", "elem"),
            P("rhs", "elem"),
        ),
        out_specs=(P("rhs", "elem"), P("rhs", "elem")),
        check_vma=False,
    )
```

```python
import jax
import jax.numpy as jnp
from jax import lax
from jax.experimental import pallas as pl
from jax.experimental.pallas import tpu as pltpu
from jax.sharding import PartitionSpec as P

DOF = 64
SLOTS = 7
QUAD = 4 * DOF
CUTS = (0, 3, 8, 16)
CHUNKS = len(CUTS) - 1
WINDOWS = 2


def masked_lanes(value, part):
    lane = lax.broadcasted_iota(jnp.int32, value.shape, 1)
    return jnp.where(lane // DOF == part, value, jnp.zeros_like(value))


def against(left, right):
    return lax.dot_general(left, right, (((1,), (1,)), ((), ())), preferred_element_type=jnp.float32)


def products(vb, panel):
    return against(jnp.concatenate([masked_lanes(vb, e) for e in range(4)], 0), panel)


def scatter(vb_ref, panel_of, cols_ref, device, windows, own_ref, stage_ref):
    width = vb_ref.shape[0]
    count = cols_ref.shape[1]
    low = lax.broadcasted_iota(jnp.int32, (width, 2 * DOF), 1) < DOF
    base = (device - 2) * count

    def multiply(quad):
        lanes = slice(quad * QUAD, (quad + 1) * QUAD)
        stage_ref[quad, :, : SLOTS * DOF] = products(vb_ref[:, lanes], panel_of(quad)[:, lanes])

    def add(quad):
        stage = stage_ref.at[quad]
        kept = None
        for e in range(4):
            rows = slice(e * width, (e + 1) * width)
            for pair in range(4):
                tile = stage[rows, pair * 2 * DOF : (pair + 1) * 2 * DOF]
                if pair == 0:
                    if e % 2 == 0:
                        kept = tile
                    else:
                        own_ref[2 * quad + e // 2] = jnp.where(low, kept, pltpu.roll(tile, DOF, 1))
                else:
                    place = cols_ref[2 * pair - 1, 4 * quad + e] - base
                    windows[0][place] += jnp.where(low, tile, 0.0)
                if pair < 3:
                    place = cols_ref[2 * pair, 4 * quad + e] - base
                    windows[1][place] += jnp.where(low, 0.0, tile)

    for quad in range(count // 4):
        multiply(quad)
        add(quad)


def sum_of(windows, place):
    total = windows[0][place]
    for window in windows[1:]:
        total = total + window[place]
    return total


def clear(windows):
    for window in windows:
        window[...] = jnp.zeros_like(window)


def hand_out(device, windows, role, out, at=0, more=None):
    half = windows[0].shape[0] // 10
    low = lax.broadcasted_iota(jnp.int32, windows[0].shape[1:], 1) < DOF
    core = lax.rem(device, 2)
    first = (core * (4 - role) + (1 - core) * role) * 2 * half
    for pair in range(half):
        even = sum_of(windows, first + 2 * pair)
        odd = sum_of(windows, first + 2 * pair + 1)
        total = jnp.where(low, even, odd) + pltpu.roll(jnp.where(low, odd, even), DOF, 1)
        out[at + pair] = total if more is None else total + more[pair]


def mate_kernel(place_ref, *refs):
    windows, (mate_ref,) = refs[:WINDOWS], refs[WINDOWS:]
    half = mate_ref.shape[0] // 2
    hand_out(place_ref[0], windows, 3, mate_ref)
    hand_out(place_ref[0], windows, 4, mate_ref, half)


def rest_kernel(place_ref, *refs):
    windows, (own_ref, near_ref, here_ref) = refs[:WINDOWS], refs[WINDOWS:]
    hand_out(place_ref[0], windows, 1, near_ref)
    hand_out(place_ref[0], windows, 2, here_ref, 0, own_ref)


def fetch(panel_hbm, panel_ref, sem):
    copies = {}
    for chunk in range(CHUNKS):
        lanes = pl.ds(CUTS[chunk] * QUAD, (CUTS[chunk + 1] - CUTS[chunk]) * QUAD)
        copies[CUTS[chunk]] = pltpu.make_async_copy(panel_hbm.at[:, lanes], panel_ref.at[:, lanes], sem.at[chunk])
    return copies


def panels(copies, panel_ref):
    def panel_of(quad):
        if quad in copies:
            copies[quad].wait()
        return panel_ref

    return panel_of


def first_kernel(place_ref, cols_hbm, panel_hbm, start_hbm, *refs):
    windows, (own_ref, far_ref, panel_ref, cols_ref, start_ref, vb_ref, stage_ref, sem) = refs[:WINDOWS], refs[WINDOWS:]
    device = place_ref[0]
    small = pltpu.make_async_copy(cols_hbm, cols_ref, sem.at[CHUNKS])
    begin = pltpu.make_async_copy(start_hbm, start_ref, sem.at[CHUNKS + 1])
    copies = fetch(panel_hbm, panel_ref, sem)
    copies[0].start()
    begin.start()
    small.start()
    for cut in CUTS[1:-1]:
        copies[cut].start()
    clear(windows)
    begin.wait()
    vb_ref[...] = start_ref[...].astype(jnp.bfloat16)
    small.wait()
    scatter(vb_ref, panels(copies, panel_ref), cols_ref, device, windows, own_ref, stage_ref)
    hand_out(device, windows, 0, far_ref)


def residual_and_update(quad, right_ref, from_ref, inv_ref, parts):
    lanes = slice(quad * QUAD, (quad + 1) * QUAD)
    sums = []
    for pair in (2 * quad, 2 * quad + 1):
        total = parts[0][pair]
        for part in parts[1:]:
            total = total + part[pair]
        sums.append(total)
    res = right_ref[:, lanes] - jnp.concatenate(sums, 1)
    resb = res.astype(jnp.bfloat16)
    spread = jnp.concatenate([masked_lanes(resb, e) for e in range(4)], 0)
    out = against(spread, inv_ref[:, lanes])
    width = res.shape[0]
    nothing = jnp.zeros((width, DOF), jnp.float32)
    each = [jnp.concatenate([out[e * width : (e + 1) * width], nothing], 1) for e in range(4)]
    update = jnp.concatenate([each[0] + pltpu.roll(each[1], DOF, 1), each[2] + pltpu.roll(each[3], DOF, 1)], 1)
    return res, from_ref[:, lanes] + update


def second_kernel(place_ref, cols_hbm, panel_ref, right_ref, start_ref, inv_ref, here_in, mate_in, far_in, near_in, *refs):
    windows, (own_ref, far_ref, first_ref, cols_ref, vb_ref, stage_ref, sem) = refs[:WINDOWS], refs[WINDOWS:]
    device = place_ref[0]
    count = cols_ref.shape[1]
    small = pltpu.make_async_copy(cols_hbm, cols_ref, sem.at[CHUNKS])
    small.start()
    clear(windows)
    for quad in range(count // 4):
        _, first = residual_and_update(quad, right_ref, start_ref, inv_ref, (here_in, mate_in, far_in, near_in))
        lanes = slice(quad * QUAD, (quad + 1) * QUAD)
        first_ref[:, lanes] = first
        vb_ref[:, lanes] = first.astype(jnp.bfloat16)
    small.wait()
    scatter(vb_ref, panels({}, panel_ref), cols_ref, device, windows, own_ref, stage_ref)
    hand_out(device, windows, 0, far_ref)


def last_kernel(right_ref, first_ref, inv_ref, here_in, mate_in, far_in, near_in, adjoint_ref, residual_ref):
    for quad in range(right_ref.shape[1] // QUAD):
        lanes = slice(quad * QUAD, (quad + 1) * QUAD)
        res, adjoint = residual_and_update(quad, right_ref, first_ref, inv_ref, (here_in, mate_in, far_in, near_in))
        residual_ref[:, lanes] = res
        adjoint_ref[:, lanes] = adjoint


VMEM = pl.BlockSpec(memory_space=pltpu.VMEM)
SMEM = pl.BlockSpec(memory_space=pltpu.SMEM)
HBM = pl.BlockSpec(memory_space=pltpu.HBM)
PARAMS = pltpu.CompilerParams(vmem_limit_bytes=40 * 1024 * 1024)


def applied(width, count):
    slab = jax.ShapeDtypeStruct((count // 2, width, 2 * DOF), jnp.float32)
    window = jax.ShapeDtypeStruct((5 * count, width, 2 * DOF), jnp.float32)
    return [window] * WINDOWS + [slab, slab]


def scratch(width, count):
    return [
        pltpu.VMEM((width, count * DOF), jnp.bfloat16),
        pltpu.VMEM((count // 4, 4 * width, 8 * DOF), jnp.float32),
        pltpu.SemaphoreType.DMA((CHUNKS + 2,)),
    ]


def in_hbm(value):
    return pltpu.with_memory_space_constraint(value, pltpu.HBM)


def exchange(place, windows, own, far, hint):
    size = lax.axis_size("elem")
    half, width, lanes = own.shape
    slab = jax.ShapeDtypeStruct(own.shape, jnp.float32)
    double = jax.ShapeDtypeStruct((2 * half, width, lanes), jnp.float32)
    outward = [(i, i + 2) for i in range(1, size - 2, 2)] + [(i, i - 2) for i in range(2, size, 2)]
    across = [(i, i + 1) for i in range(1, size - 1, 2)] + [(i + 1, i) for i in range(1, size - 1, 2)]
    far = lax.ppermute(far, "elem", outward)
    mate = pl.pallas_call(
        mate_kernel,
        out_shape=double,
        in_specs=[SMEM] + [VMEM] * WINDOWS,
        out_specs=VMEM,
        compiler_params=PARAMS,
        cost_estimate=pl.CostEstimate(flops=10**8, bytes_accessed=4 * 10**6, transcendentals=0),
    )(place, *windows)
    mate = lax.ppermute(mate, "elem", [(i, i ^ 1) for i in range(size)])
    near, here = pl.pallas_call(
        rest_kernel,
        out_shape=[slab, slab],
        in_specs=[SMEM] + [VMEM] * (WINDOWS + 1),
        out_specs=[VMEM, VMEM],
        compiler_params=PARAMS,
        cost_estimate=pl.CostEstimate(flops=hint, bytes_accessed=4 * 10**6, transcendentals=0),
    )(place, *windows, own)
    near = lax.ppermute(near + mate[half:], "elem", across)
    return here, mate[:half], far, near


def body(blocks, cols, inverse, right_side, start):
    width = start.shape[0]
    count = cols.shape[1]
    place = lax.axis_index("elem").astype(jnp.int32).reshape(1)
    out = jax.ShapeDtypeStruct(start.shape, jnp.float32)
    cols = in_hbm(cols)
    *windows, own, far, panel = pl.pallas_call(
        first_kernel,
        out_shape=applied(width, count) + [pltpu.VMEM(blocks.shape[::-1], jnp.bfloat16)],
        in_specs=[SMEM, HBM, HBM, HBM],
        out_specs=[VMEM] * (WINDOWS + 3),
        scratch_shapes=[pltpu.SMEM(cols.shape, jnp.int32), pltpu.VMEM(start.shape, jnp.float32)] + scratch(width, count),
        compiler_params=PARAMS,
    )(place, cols, in_hbm(blocks.T), in_hbm(start))
    parts = exchange(place, windows, own, far, 10**8)
    *windows, own, far, first = pl.pallas_call(
        second_kernel,
        out_shape=applied(width, count) + [out],
        in_specs=[SMEM, HBM] + [VMEM] * 8,
        out_specs=[VMEM] * (WINDOWS + 3),
        scratch_shapes=[pltpu.SMEM(cols.shape, jnp.int32)] + scratch(width, count),
        compiler_params=PARAMS,
    )(place, cols, panel, right_side, start, inverse, *parts)
    parts = exchange(place, windows, own, far, 10**10)
    adjoint, residual = pl.pallas_call(
        last_kernel,
        out_shape=[out, out],
        in_specs=[VMEM] * 7,
        out_specs=[VMEM] * 2,
        compiler_params=PARAMS,
    )(right_side, first, inverse, *parts)
    return (adjoint, residual)


def solution(mesh):
    return jax.shard_map(
        body,
        mesh=mesh,
        in_specs=(
            P("elem", None),
            P(None, "elem"),
            P(None, "elem"),
            P("rhs", "elem"),
            P("rhs", "elem"),
        ),
        out_specs=(P("rhs", "elem"), P("rhs", "elem")),
        check_vma=False,
    )
```

```python
import jax
import jax.numpy as jnp
from jax import lax
from jax.experimental import pallas as pl
from jax.experimental.pallas import tpu as pltpu
from jax.sharding import PartitionSpec as P

DOF = 64
SLOTS = 7
QUAD = 4 * DOF
CUTS = (0, 3, 8, 16)
CHUNKS = len(CUTS) - 1
WINDOWS = 2


def masked_lanes(value, part):
    lane = lax.broadcasted_iota(jnp.int32, value.shape, 1)
    return jnp.where(lane // DOF == part, value, jnp.zeros_like(value))


def against(left, right):
    return lax.dot_general(left, right, (((1,), (1,)), ((), ())), preferred_element_type=jnp.float32)


def products(vb, panel):
    return against(jnp.concatenate([masked_lanes(vb, e) for e in range(4)], 0), panel)


def scatter(vb_ref, panel_of, cols_ref, device, windows, own_ref, stage_ref):
    width = vb_ref.shape[0]
    count = cols_ref.shape[1]
    low = lax.broadcasted_iota(jnp.int32, (width, 2 * DOF), 1) < DOF
    base = (device - 2) * count

    def multiply(quad):
        lanes = slice(quad * QUAD, (quad + 1) * QUAD)
        stage_ref[quad, :, : SLOTS * DOF] = products(vb_ref[:, lanes], panel_of(quad)[:, lanes])

    def add(quad):
        stage = stage_ref.at[quad]
        kept = None
        for e in range(4):
            rows = slice(e * width, (e + 1) * width)
            for pair in range(4):
                tile = stage[rows, pair * 2 * DOF : (pair + 1) * 2 * DOF]
                if pair == 0:
                    if e % 2 == 0:
                        kept = tile
                    else:
                        own_ref[2 * quad + e // 2] = jnp.where(low, kept, pltpu.roll(tile, DOF, 1))
                else:
                    place = cols_ref[2 * pair - 1, 4 * quad + e] - base
                    windows[0][place] += tile
                if pair < 3:
                    place = cols_ref[2 * pair, 4 * quad + e] - base
                    windows[1][place] += tile

    for quad in range(count // 4):
        multiply(quad)
        add(quad)


def clear(windows):
    for window in windows:
        window[...] = jnp.zeros_like(window)


def hand_out(device, windows, role, out, at=0, more=None):
    half = windows[0].shape[0] // 10
    low = lax.broadcasted_iota(jnp.int32, windows[0].shape[1:], 1) < DOF
    core = lax.rem(device, 2)
    first = (core * (4 - role) + (1 - core) * role) * 2 * half
    for pair in range(half):
        here, next_one = first + 2 * pair, first + 2 * pair + 1
        kept = jnp.where(low, windows[0][here], windows[1][next_one])
        crossed = jnp.where(low, windows[0][next_one], windows[1][here])
        total = kept + pltpu.roll(crossed, DOF, 1)
        out[at + pair] = total if more is None else total + more[pair]


def mate_kernel(place_ref, *refs):
    windows, (mate_ref,) = refs[:WINDOWS], refs[WINDOWS:]
    half = mate_ref.shape[0] // 2
    hand_out(place_ref[0], windows, 3, mate_ref)
    hand_out(place_ref[0], windows, 4, mate_ref, half)


def clearing_kernel(place_ref, *refs):
    (own_ref, near_ref, here_ref), windows = refs[WINDOWS : WINDOWS + 3], refs[WINDOWS + 3 :]
    hand_out(place_ref[0], windows, 1, near_ref)
    hand_out(place_ref[0], windows, 2, here_ref, 0, own_ref)
    clear(windows)


def rest_kernel(place_ref, *refs):
    windows, (own_ref, near_ref, here_ref) = refs[:WINDOWS], refs[WINDOWS:]
    hand_out(place_ref[0], windows, 1, near_ref)
    hand_out(place_ref[0], windows, 2, here_ref, 0, own_ref)


def fetch(panel_hbm, panel_ref, sem):
    copies = {}
    for chunk in range(CHUNKS):
        lanes = pl.ds(CUTS[chunk] * QUAD, (CUTS[chunk + 1] - CUTS[chunk]) * QUAD)
        copies[CUTS[chunk]] = pltpu.make_async_copy(panel_hbm.at[:, lanes], panel_ref.at[:, lanes], sem.at[chunk])
    return copies


def panels(copies, panel_ref):
    def panel_of(quad):
        if quad in copies:
            copies[quad].wait()
        return panel_ref

    return panel_of


def first_kernel(place_ref, cols_hbm, panel_hbm, start_hbm, *refs):
    windows, (own_ref, far_ref, mate_ref, panel_ref, cols_ref, start_ref, vb_ref, stage_ref, sem) = refs[:WINDOWS], refs[WINDOWS:]
    device = place_ref[0]
    small = pltpu.make_async_copy(cols_hbm, cols_ref, sem.at[CHUNKS])
    begin = pltpu.make_async_copy(start_hbm, start_ref, sem.at[CHUNKS + 1])
    copies = fetch(panel_hbm, panel_ref, sem)
    copies[0].start()
    begin.start()
    small.start()
    for cut in CUTS[1:-1]:
        copies[cut].start()
    clear(windows)
    begin.wait()
    vb_ref[...] = start_ref[...].astype(jnp.bfloat16)
    small.wait()
    scatter(vb_ref, panels(copies, panel_ref), cols_ref, device, windows, own_ref, stage_ref)
    hand_out(device, windows, 0, far_ref)
    hand_out(device, windows, 3, mate_ref)
    hand_out(device, windows, 4, mate_ref, mate_ref.shape[0] // 2)


def residual_and_update(quad, right_ref, from_ref, inv_ref, parts):
    lanes = slice(quad * QUAD, (quad + 1) * QUAD)
    sums = []
    for pair in (2 * quad, 2 * quad + 1):
        total = parts[0][pair]
        for part in parts[1:]:
            total = total + part[pair]
        sums.append(total)
    res = right_ref[:, lanes] - jnp.concatenate(sums, 1)
    resb = res.astype(jnp.bfloat16)
    spread = jnp.concatenate([masked_lanes(resb, e) for e in range(4)], 0)
    out = against(spread, inv_ref[:, lanes])
    width = res.shape[0]
    nothing = jnp.zeros((width, DOF), jnp.float32)
    each = [jnp.concatenate([out[e * width : (e + 1) * width], nothing], 1) for e in range(4)]
    update = jnp.concatenate([each[0] + pltpu.roll(each[1], DOF, 1), each[2] + pltpu.roll(each[3], DOF, 1)], 1)
    return res, from_ref[:, lanes] + update


def second_kernel(place_ref, cols_hbm, panel_ref, right_ref, start_ref, inv_ref, here_in, mate_in, far_in, near_in, *refs):
    refs = refs[WINDOWS:]
    windows, (own_ref, far_ref, first_ref, cols_ref, vb_ref, stage_ref, sem) = refs[:WINDOWS], refs[WINDOWS:]
    device = place_ref[0]
    count = cols_ref.shape[1]
    small = pltpu.make_async_copy(cols_hbm, cols_ref, sem.at[CHUNKS])
    small.start()
    for quad in range(count // 4):
        _, first = residual_and_update(quad, right_ref, start_ref, inv_ref, (here_in, mate_in, far_in, near_in))
        lanes = slice(quad * QUAD, (quad + 1) * QUAD)
        first_ref[:, lanes] = first
        vb_ref[:, lanes] = first.astype(jnp.bfloat16)
    small.wait()
    scatter(vb_ref, panels({}, panel_ref), cols_ref, device, windows, own_ref, stage_ref)
    hand_out(device, windows, 0, far_ref)


def last_kernel(right_ref, first_ref, inv_ref, here_in, mate_in, far_in, near_in, adjoint_ref, residual_ref):
    for quad in range(right_ref.shape[1] // QUAD):
        lanes = slice(quad * QUAD, (quad + 1) * QUAD)
        res, adjoint = residual_and_update(quad, right_ref, first_ref, inv_ref, (here_in, mate_in, far_in, near_in))
        residual_ref[:, lanes] = res
        adjoint_ref[:, lanes] = adjoint


VMEM = pl.BlockSpec(memory_space=pltpu.VMEM)
SMEM = pl.BlockSpec(memory_space=pltpu.SMEM)
HBM = pl.BlockSpec(memory_space=pltpu.HBM)
PARAMS = pltpu.CompilerParams(vmem_limit_bytes=40 * 1024 * 1024)


def applied(width, count):
    slab = jax.ShapeDtypeStruct((count // 2, width, 2 * DOF), jnp.float32)
    window = jax.ShapeDtypeStruct((5 * count, width, 2 * DOF), jnp.float32)
    return [window] * WINDOWS + [slab, slab]


def scratch(width, count):
    return [
        pltpu.VMEM((width, count * DOF), jnp.bfloat16),
        pltpu.VMEM((count // 4, 4 * width, 8 * DOF), jnp.float32),
        pltpu.SemaphoreType.DMA((CHUNKS + 2,)),
    ]


def in_hbm(value):
    return pltpu.with_memory_space_constraint(value, pltpu.HBM)


def mate_slabs(place, windows, own):
    half, width, lanes = own.shape
    return pl.pallas_call(
        mate_kernel,
        out_shape=jax.ShapeDtypeStruct((2 * half, width, lanes), jnp.float32),
        in_specs=[SMEM] + [VMEM] * WINDOWS,
        out_specs=VMEM,
        compiler_params=PARAMS,
        cost_estimate=pl.CostEstimate(flops=10**8, bytes_accessed=4 * 10**6, transcendentals=0),
    )(place, *windows)


def exchange(place, windows, own, far, mate, hint, again):
    size = lax.axis_size("elem")
    half = own.shape[0]
    slab = jax.ShapeDtypeStruct(own.shape, jnp.float32)
    outward = [(i, i + 2) for i in range(1, size - 2, 2)] + [(i, i - 2) for i in range(2, size, 2)]
    across = [(i, i + 1) for i in range(1, size - 1, 2)] + [(i + 1, i) for i in range(1, size - 1, 2)]
    far = lax.ppermute(far, "elem", outward)
    mate = lax.ppermute(mate, "elem", [(i, i ^ 1) for i in range(size)])
    near, here, *windows = pl.pallas_call(
        clearing_kernel if again else rest_kernel,
        out_shape=[slab, slab] + [jax.ShapeDtypeStruct(w.shape, w.dtype) for w in windows if again],
        in_specs=[SMEM] + [VMEM] * (WINDOWS + 1),
        out_specs=[VMEM] * (2 + WINDOWS * again),
        input_output_aliases={1 + i: 2 + i for i in range(WINDOWS * again)},
        compiler_params=PARAMS,
        cost_estimate=pl.CostEstimate(flops=hint, bytes_accessed=4 * 10**6, transcendentals=0),
    )(place, *windows, own)
    near = lax.ppermute(near + mate[half:], "elem", across)
    return (here, mate[:half], far, near), windows


def body(blocks, cols, inverse, right_side, start):
    width = start.shape[0]
    count = cols.shape[1]
    place = lax.axis_index("elem").astype(jnp.int32).reshape(1)
    out = jax.ShapeDtypeStruct(start.shape, jnp.float32)
    double = jax.ShapeDtypeStruct((count, width, 2 * DOF), jnp.float32)
    cols = in_hbm(cols)
    *windows, own, far, mate, panel = pl.pallas_call(
        first_kernel,
        out_shape=applied(width, count) + [double, pltpu.VMEM(blocks.shape[::-1], jnp.bfloat16)],
        in_specs=[SMEM, HBM, HBM, HBM],
        out_specs=[VMEM] * (WINDOWS + 4),
        scratch_shapes=[pltpu.SMEM(cols.shape, jnp.int32), pltpu.VMEM(start.shape, jnp.float32)] + scratch(width, count),
        compiler_params=PARAMS,
    )(place, cols, in_hbm(blocks.T), in_hbm(start))
    parts, windows = exchange(place, windows, own, far, mate, 10**8, True)
    *windows, own, far, first = pl.pallas_call(
        second_kernel,
        out_shape=applied(width, count) + [out],
        in_specs=[SMEM, HBM] + [VMEM] * (8 + WINDOWS),
        input_output_aliases={10 + i: i for i in range(WINDOWS)},
        out_specs=[VMEM] * (WINDOWS + 3),
        scratch_shapes=[pltpu.SMEM(cols.shape, jnp.int32)] + scratch(width, count),
        compiler_params=PARAMS,
    )(place, cols, panel, right_side, start, inverse, *parts, *windows)
    parts, _ = exchange(place, windows, own, far, mate_slabs(place, windows, own), 10**10, False)
    adjoint, residual = pl.pallas_call(
        last_kernel,
        out_shape=[out, out],
        in_specs=[VMEM] * 7,
        out_specs=[VMEM] * 2,
        compiler_params=PARAMS,
    )(right_side, first, inverse, *parts)
    return (adjoint, residual)


def solution(mesh):
    return jax.shard_map(
        body,
        mesh=mesh,
        in_specs=(
            P("elem", None),
            P(None, "elem"),
            P(None, "elem"),
            P("rhs", "elem"),
            P("rhs", "elem"),
        ),
        out_specs=(P("rhs", "elem"), P("rhs", "elem")),
        check_vma=False,
    )
```

```python
import jax
import jax.numpy as jnp
from jax import lax
from jax.experimental import pallas as pl
from jax.experimental.pallas import tpu as pltpu
from jax.sharding import PartitionSpec as P

DOF = 64
SLOTS = 7
QUAD = 4 * DOF
CUTS = (0, 3, 8, 16)
CHUNKS = len(CUTS) - 1
WINDOWS = 2


def masked_lanes(value, part):
    lane = lax.broadcasted_iota(jnp.int32, value.shape, 1)
    return jnp.where(lane // DOF == part, value, jnp.zeros_like(value))


def against(left, right):
    return lax.dot_general(left, right, (((1,), (1,)), ((), ())), preferred_element_type=jnp.float32)


def products(vb, panel):
    return against(jnp.concatenate([masked_lanes(vb, e) for e in range(4)], 0), panel)


def scatter(vb_ref, panel_of, cols_ref, device, windows, own_ref, stage_ref):
    width = vb_ref.shape[0]
    count = cols_ref.shape[1]
    low = lax.broadcasted_iota(jnp.int32, (width, 2 * DOF), 1) < DOF
    base = (device - 2) * count

    def multiply(quad):
        lanes = slice(quad * QUAD, (quad + 1) * QUAD)
        stage_ref[quad, :, : SLOTS * DOF] = products(vb_ref[:, lanes], panel_of(quad)[:, lanes])

    def add(quad):
        stage = stage_ref.at[quad]
        kept = None
        for e in range(4):
            rows = slice(e * width, (e + 1) * width)
            for pair in range(4):
                tile = stage[rows, pair * 2 * DOF : (pair + 1) * 2 * DOF]
                if pair == 0:
                    if e % 2 == 0:
                        kept = tile
                    else:
                        own_ref[2 * quad + e // 2] = jnp.where(low, kept, pltpu.roll(tile, DOF, 1))
                else:
                    place = cols_ref[2 * pair - 1, 4 * quad + e] - base
                    windows[0][place] += tile
                if pair < 3:
                    place = cols_ref[2 * pair, 4 * quad + e] - base
                    windows[1][place] += tile

    for quad in range(count // 4):
        multiply(quad)
        add(quad)


def clear(windows):
    for window in windows:
        window[...] = jnp.zeros_like(window)


def hand_out(device, windows, role, out, at=0, more=None):
    half = windows[0].shape[0] // 10
    low = lax.broadcasted_iota(jnp.int32, windows[0].shape[1:], 1) < DOF
    core = lax.rem(device, 2)
    first = (core * (4 - role) + (1 - core) * role) * 2 * half
    for pair in range(half):
        here, next_one = first + 2 * pair, first + 2 * pair + 1
        kept = jnp.where(low, windows[0][here], windows[1][next_one])
        crossed = jnp.where(low, windows[0][next_one], windows[1][here])
        total = kept + pltpu.roll(crossed, DOF, 1)
        out[at + pair] = total if more is None else total + more[pair]


def mate_kernel(place_ref, *refs):
    windows, (mate_ref,) = refs[:WINDOWS], refs[WINDOWS:]
    half = mate_ref.shape[0] // 2
    hand_out(place_ref[0], windows, 3, mate_ref)
    hand_out(place_ref[0], windows, 4, mate_ref, half)


def here_kernel(place_ref, *refs):
    windows, (own_ref, far_in, here_ref) = refs[:WINDOWS], refs[WINDOWS:]
    hand_out(place_ref[0], windows, 2, here_ref, 0, own_ref)
    here_ref[...] += far_in[...]


def rest_kernel(place_ref, *refs):
    windows, (own_ref, near_ref, here_ref) = refs[:WINDOWS], refs[WINDOWS:]
    hand_out(place_ref[0], windows, 1, near_ref)
    hand_out(place_ref[0], windows, 2, here_ref, 0, own_ref)


def fetch(panel_hbm, panel_ref, sem):
    copies = {}
    for chunk in range(CHUNKS):
        lanes = pl.ds(CUTS[chunk] * QUAD, (CUTS[chunk + 1] - CUTS[chunk]) * QUAD)
        copies[CUTS[chunk]] = pltpu.make_async_copy(panel_hbm.at[:, lanes], panel_ref.at[:, lanes], sem.at[chunk])
    return copies


def panels(copies, panel_ref):
    def panel_of(quad):
        if quad in copies:
            copies[quad].wait()
        return panel_ref

    return panel_of


def first_kernel(place_ref, cols_hbm, panel_hbm, start_hbm, *refs):
    windows, (own_ref, far_ref, mate_ref, near_ref, panel_ref, cols_ref, start_ref, vb_ref, stage_ref, sem) = refs[:WINDOWS], refs[WINDOWS:]
    device = place_ref[0]
    small = pltpu.make_async_copy(cols_hbm, cols_ref, sem.at[CHUNKS])
    begin = pltpu.make_async_copy(start_hbm, start_ref, sem.at[CHUNKS + 1])
    copies = fetch(panel_hbm, panel_ref, sem)
    copies[0].start()
    begin.start()
    small.start()
    for cut in CUTS[1:-1]:
        copies[cut].start()
    clear(windows)
    begin.wait()
    vb_ref[...] = start_ref[...].astype(jnp.bfloat16)
    small.wait()
    scatter(vb_ref, panels(copies, panel_ref), cols_ref, device, windows, own_ref, stage_ref)
    hand_out(device, windows, 0, far_ref)
    hand_out(device, windows, 3, mate_ref)
    hand_out(device, windows, 4, mate_ref, mate_ref.shape[0] // 2)
    hand_out(device, windows, 1, near_ref)


def residual_and_update(quad, right_ref, from_ref, inv_ref, parts):
    lanes = slice(quad * QUAD, (quad + 1) * QUAD)
    sums = []
    for pair in (2 * quad, 2 * quad + 1):
        total = parts[0][pair]
        for part in parts[1:]:
            total = total + part[pair]
        sums.append(total)
    res = right_ref[:, lanes] - jnp.concatenate(sums, 1)
    resb = res.astype(jnp.bfloat16)
    spread = jnp.concatenate([masked_lanes(resb, e) for e in range(4)], 0)
    out = against(spread, inv_ref[:, lanes])
    width = res.shape[0]
    nothing = jnp.zeros((width, DOF), jnp.float32)
    each = [jnp.concatenate([out[e * width : (e + 1) * width], nothing], 1) for e in range(4)]
    update = jnp.concatenate([each[0] + pltpu.roll(each[1], DOF, 1), each[2] + pltpu.roll(each[3], DOF, 1)], 1)
    return res, from_ref[:, lanes] + update


def second_kernel(place_ref, cols_hbm, panel_ref, right_ref, start_ref, inv_ref, here_in, mate_in, near_in, *refs):
    windows, (own_ref, far_ref, first_ref, cols_ref, vb_ref, stage_ref, sem) = refs[:WINDOWS], refs[WINDOWS:]
    device = place_ref[0]
    count = cols_ref.shape[1]
    small = pltpu.make_async_copy(cols_hbm, cols_ref, sem.at[CHUNKS])
    small.start()
    clear(windows)
    for quad in range(count // 4):
        _, first = residual_and_update(quad, right_ref, start_ref, inv_ref, (here_in, mate_in, near_in))
        lanes = slice(quad * QUAD, (quad + 1) * QUAD)
        first_ref[:, lanes] = first
        vb_ref[:, lanes] = first.astype(jnp.bfloat16)
    small.wait()
    scatter(vb_ref, panels({}, panel_ref), cols_ref, device, windows, own_ref, stage_ref)
    hand_out(device, windows, 0, far_ref)


def last_kernel(right_ref, first_ref, inv_ref, here_in, mate_in, far_in, near_in, adjoint_ref, residual_ref):
    for quad in range(right_ref.shape[1] // QUAD):
        lanes = slice(quad * QUAD, (quad + 1) * QUAD)
        res, adjoint = residual_and_update(quad, right_ref, first_ref, inv_ref, (here_in, mate_in, far_in, near_in))
        residual_ref[:, lanes] = res
        adjoint_ref[:, lanes] = adjoint


VMEM = pl.BlockSpec(memory_space=pltpu.VMEM)
SMEM = pl.BlockSpec(memory_space=pltpu.SMEM)
HBM = pl.BlockSpec(memory_space=pltpu.HBM)
PARAMS = pltpu.CompilerParams(vmem_limit_bytes=40 * 1024 * 1024)


def applied(width, count):
    slab = jax.ShapeDtypeStruct((count // 2, width, 2 * DOF), jnp.float32)
    window = jax.ShapeDtypeStruct((5 * count, width, 2 * DOF), jnp.float32)
    return [window] * WINDOWS + [slab, slab]


def scratch(width, count):
    return [
        pltpu.VMEM((width, count * DOF), jnp.bfloat16),
        pltpu.VMEM((count // 4, 4 * width, 8 * DOF), jnp.float32),
        pltpu.SemaphoreType.DMA((CHUNKS + 2,)),
    ]


def in_hbm(value):
    return pltpu.with_memory_space_constraint(value, pltpu.HBM)


def mate_slabs(place, windows, own):
    half, width, lanes = own.shape
    return pl.pallas_call(
        mate_kernel,
        out_shape=jax.ShapeDtypeStruct((2 * half, width, lanes), jnp.float32),
        in_specs=[SMEM] + [VMEM] * WINDOWS,
        out_specs=VMEM,
        compiler_params=PARAMS,
        cost_estimate=pl.CostEstimate(flops=10**8, bytes_accessed=4 * 10**6, transcendentals=0),
    )(place, *windows)


def pairs(size):
    outward = [(i, i + 2) for i in range(1, size - 2, 2)] + [(i, i - 2) for i in range(2, size, 2)]
    across = [(i, i + 1) for i in range(1, size - 1, 2)] + [(i + 1, i) for i in range(1, size - 1, 2)]
    return outward, [(i, i ^ 1) for i in range(size)], across


def slab_call(kernel, place, operands, outs, hint):
    slab = jax.ShapeDtypeStruct(operands[WINDOWS].shape, jnp.float32)
    return pl.pallas_call(
        kernel,
        out_shape=[slab] * outs,
        in_specs=[SMEM] + [VMEM] * len(operands),
        out_specs=[VMEM] * outs,
        compiler_params=PARAMS,
        cost_estimate=pl.CostEstimate(flops=hint, bytes_accessed=4 * 10**6, transcendentals=0),
    )(place, *operands)


def first_exchange(place, windows, own, far, mate, near):
    outward, swapped, across = pairs(lax.axis_size("elem"))
    half = own.shape[0]
    far = lax.ppermute(far, "elem", outward)
    mate = lax.ppermute(mate, "elem", swapped)
    near = lax.ppermute(near + mate[half:], "elem", across)
    (here,) = slab_call(here_kernel, place, (*windows, own, far), 1, 10**8)
    return here, mate[:half], near


def second_exchange(place, windows, own, far):
    outward, swapped, across = pairs(lax.axis_size("elem"))
    half = own.shape[0]
    far = lax.ppermute(far, "elem", outward)
    mate = lax.ppermute(mate_slabs(place, windows, own), "elem", swapped)
    near, here = slab_call(rest_kernel, place, (*windows, own), 2, 10**10)
    near = lax.ppermute(near + mate[half:], "elem", across)
    return here, mate[:half], far, near


def body(blocks, cols, inverse, right_side, start):
    width = start.shape[0]
    count = cols.shape[1]
    place = lax.axis_index("elem").astype(jnp.int32).reshape(1)
    out = jax.ShapeDtypeStruct(start.shape, jnp.float32)
    double = jax.ShapeDtypeStruct((count, width, 2 * DOF), jnp.float32)
    slab = jax.ShapeDtypeStruct((count // 2, width, 2 * DOF), jnp.float32)
    cols = in_hbm(cols)
    *windows, own, far, mate, near, panel = pl.pallas_call(
        first_kernel,
        out_shape=applied(width, count) + [double, slab, pltpu.VMEM(blocks.shape[::-1], jnp.bfloat16)],
        in_specs=[SMEM, HBM, HBM, HBM],
        out_specs=[VMEM] * (WINDOWS + 5),
        scratch_shapes=[pltpu.SMEM(cols.shape, jnp.int32), pltpu.VMEM(start.shape, jnp.float32)] + scratch(width, count),
        compiler_params=PARAMS,
    )(place, cols, in_hbm(blocks.T), in_hbm(start))
    parts = first_exchange(place, windows, own, far, mate, near)
    *windows, own, far, first = pl.pallas_call(
        second_kernel,
        out_shape=applied(width, count) + [out],
        in_specs=[SMEM, HBM] + [VMEM] * 7,
        out_specs=[VMEM] * (WINDOWS + 3),
        scratch_shapes=[pltpu.SMEM(cols.shape, jnp.int32)] + scratch(width, count),
        compiler_params=PARAMS,
    )(place, cols, panel, right_side, start, inverse, *parts)
    parts = second_exchange(place, windows, own, far)
    adjoint, residual = pl.pallas_call(
        last_kernel,
        out_shape=[out, out],
        in_specs=[VMEM] * 7,
        out_specs=[VMEM] * 2,
        compiler_params=PARAMS,
    )(right_side, first, inverse, *parts)
    return (adjoint, residual)


def solution(mesh):
    return jax.shard_map(
        body,
        mesh=mesh,
        in_specs=(
            P("elem", None),
            P(None, "elem"),
            P(None, "elem"),
            P("rhs", "elem"),
            P("rhs", "elem"),
        ),
        out_specs=(P("rhs", "elem"), P("rhs", "elem")),
        check_vma=False,
    )
```

```python
import jax
import jax.numpy as jnp
from jax import lax
from jax.experimental import pallas as pl
from jax.experimental.pallas import tpu as pltpu
from jax.sharding import PartitionSpec as P

DOF = 64
SLOTS = 7
QUAD = 4 * DOF
CUTS = (0, 3, 8, 16)
CHUNKS = len(CUTS) - 1
WINDOWS = 2


def masked_lanes(value, part):
    lane = lax.broadcasted_iota(jnp.int32, value.shape, 1)
    return jnp.where(lane // DOF == part, value, jnp.zeros_like(value))


def against(left, right):
    return lax.dot_general(left, right, (((1,), (1,)), ((), ())), preferred_element_type=jnp.float32)


def products(vb, panel):
    return against(jnp.concatenate([masked_lanes(vb, e) for e in range(4)], 0), panel)


def scatter(vb_ref, panel_of, cols_ref, device, windows, own_ref, stage_ref, uncleared=()):
    width = vb_ref.shape[0]
    count = cols_ref.shape[1]
    low = lax.broadcasted_iota(jnp.int32, (width, 2 * DOF), 1) < DOF
    base = (device - 2) * count

    def multiply(quad):
        lanes = slice(quad * QUAD, (quad + 1) * QUAD)
        stage_ref[quad, :, : SLOTS * DOF] = products(vb_ref[:, lanes], panel_of(quad)[:, lanes])

    def add(quad):
        stage = stage_ref.at[quad]
        kept = None
        for e in range(4):
            rows = slice(e * width, (e + 1) * width)
            for pair in range(4):
                tile = stage[rows, pair * 2 * DOF : (pair + 1) * 2 * DOF]
                if pair == 0:
                    if e % 2 == 0:
                        kept = tile
                    else:
                        own_ref[2 * quad + e // 2] = jnp.where(low, kept, pltpu.roll(tile, DOF, 1))
                else:
                    place = cols_ref[2 * pair - 1, 4 * quad + e] - base
                    windows[0][place] += jnp.where(low, tile, 0.0)
                if pair < 3:
                    place = cols_ref[2 * pair, 4 * quad + e] - base
                    windows[1][place] += jnp.where(low, 0.0, tile)

    for quad in range(count // 4):
        multiply(quad)
        if quad == 0:
            clear(uncleared)
        add(quad)


def sum_of(windows, place):
    total = windows[0][place]
    for window in windows[1:]:
        total = total + window[place]
    return total


def clear(windows):
    for window in windows:
        window[...] = jnp.zeros_like(window)


def hand_out(device, windows, role, out, at=0, more=None):
    half = windows[0].shape[0] // 10
    low = lax.broadcasted_iota(jnp.int32, windows[0].shape[1:], 1) < DOF
    core = lax.rem(device, 2)
    first = (core * (4 - role) + (1 - core) * role) * 2 * half
    for pair in range(half):
        even = sum_of(windows, first + 2 * pair)
        odd = sum_of(windows, first + 2 * pair + 1)
        total = jnp.where(low, even, odd) + pltpu.roll(jnp.where(low, odd, even), DOF, 1)
        out[at + pair] = total if more is None else total + more[pair]


def mate_kernel(place_ref, *refs):
    windows, (mate_ref,) = refs[:WINDOWS], refs[WINDOWS:]
    half = mate_ref.shape[0] // 2
    hand_out(place_ref[0], windows, 3, mate_ref)
    hand_out(place_ref[0], windows, 4, mate_ref, half)


def rest_kernel(place_ref, *refs):
    windows, (own_ref, near_ref, here_ref) = refs[:WINDOWS], refs[WINDOWS:]
    hand_out(place_ref[0], windows, 1, near_ref)
    hand_out(place_ref[0], windows, 2, here_ref, 0, own_ref)


def fetch(panel_hbm, panel_ref, sem):
    copies = {}
    for chunk in range(CHUNKS):
        lanes = pl.ds(CUTS[chunk] * QUAD, (CUTS[chunk + 1] - CUTS[chunk]) * QUAD)
        copies[CUTS[chunk]] = pltpu.make_async_copy(panel_hbm.at[:, lanes], panel_ref.at[:, lanes], sem.at[chunk])
    return copies


def panels(copies, panel_ref):
    def panel_of(quad):
        if quad in copies:
            copies[quad].wait()
        return panel_ref

    return panel_of


def first_kernel(place_ref, cols_hbm, panel_hbm, start_hbm, *refs):
    windows, (own_ref, far_ref, panel_ref, cols_ref, start_ref, vb_ref, stage_ref, sem) = refs[:WINDOWS], refs[WINDOWS:]
    device = place_ref[0]
    small = pltpu.make_async_copy(cols_hbm, cols_ref, sem.at[CHUNKS])
    begin = pltpu.make_async_copy(start_hbm, start_ref, sem.at[CHUNKS + 1])
    copies = fetch(panel_hbm, panel_ref, sem)
    copies[0].start()
    begin.start()
    small.start()
    for cut in CUTS[1:-1]:
        copies[cut].start()
    clear(windows[1:])
    begin.wait()
    vb_ref[...] = start_ref[...].astype(jnp.bfloat16)
    small.wait()
    scatter(vb_ref, panels(copies, panel_ref), cols_ref, device, windows, own_ref, stage_ref, windows[:1])
    hand_out(device, windows, 0, far_ref)


def residual_and_update(quad, right_ref, from_ref, inv_ref, parts):
    lanes = slice(quad * QUAD, (quad + 1) * QUAD)
    sums = []
    for pair in (2 * quad, 2 * quad + 1):
        total = parts[0][pair]
        for part in parts[1:]:
            total = total + part[pair]
        sums.append(total)
    res = right_ref[:, lanes] - jnp.concatenate(sums, 1)
    resb = res.astype(jnp.bfloat16)
    spread = jnp.concatenate([masked_lanes(resb, e) for e in range(4)], 0)
    out = against(spread, inv_ref[:, lanes])
    width = res.shape[0]
    nothing = jnp.zeros((width, DOF), jnp.float32)
    each = [jnp.concatenate([out[e * width : (e + 1) * width], nothing], 1) for e in range(4)]
    update = jnp.concatenate([each[0] + pltpu.roll(each[1], DOF, 1), each[2] + pltpu.roll(each[3], DOF, 1)], 1)
    return res, from_ref[:, lanes] + update


def second_kernel(place_ref, cols_hbm, panel_ref, right_ref, start_ref, inv_ref, here_in, mate_in, far_in, near_in, *refs):
    windows, (own_ref, far_ref, first_ref, cols_ref, vb_ref, stage_ref, sem) = refs[:WINDOWS], refs[WINDOWS:]
    device = place_ref[0]
    count = cols_ref.shape[1]
    small = pltpu.make_async_copy(cols_hbm, cols_ref, sem.at[CHUNKS])
    small.start()
    clear(windows)
    for quad in range(count // 4):
        _, first = residual_and_update(quad, right_ref, start_ref, inv_ref, (here_in, mate_in, far_in, near_in))
        lanes = slice(quad * QUAD, (quad + 1) * QUAD)
        first_ref[:, lanes] = first
        vb_ref[:, lanes] = first.astype(jnp.bfloat16)
    small.wait()
    scatter(vb_ref, panels({}, panel_ref), cols_ref, device, windows, own_ref, stage_ref)
    hand_out(device, windows, 0, far_ref)


def last_kernel(right_ref, first_ref, inv_ref, here_in, mate_in, far_in, near_in, adjoint_ref, residual_ref):
    for quad in range(right_ref.shape[1] // QUAD):
        lanes = slice(quad * QUAD, (quad + 1) * QUAD)
        res, adjoint = residual_and_update(quad, right_ref, first_ref, inv_ref, (here_in, mate_in, far_in, near_in))
        residual_ref[:, lanes] = res
        adjoint_ref[:, lanes] = adjoint


VMEM = pl.BlockSpec(memory_space=pltpu.VMEM)
SMEM = pl.BlockSpec(memory_space=pltpu.SMEM)
HBM = pl.BlockSpec(memory_space=pltpu.HBM)
PARAMS = pltpu.CompilerParams(vmem_limit_bytes=40 * 1024 * 1024)


def applied(width, count):
    slab = jax.ShapeDtypeStruct((count // 2, width, 2 * DOF), jnp.float32)
    window = jax.ShapeDtypeStruct((5 * count, width, 2 * DOF), jnp.float32)
    return [window] * WINDOWS + [slab, slab]


def scratch(width, count):
    return [
        pltpu.VMEM((width, count * DOF), jnp.bfloat16),
        pltpu.VMEM((count // 4, 4 * width, 8 * DOF), jnp.float32),
        pltpu.SemaphoreType.DMA((CHUNKS + 2,)),
    ]


def in_hbm(value):
    return pltpu.with_memory_space_constraint(value, pltpu.HBM)


def exchange(place, windows, own, far, hint):
    size = lax.axis_size("elem")
    half, width, lanes = own.shape
    slab = jax.ShapeDtypeStruct(own.shape, jnp.float32)
    double = jax.ShapeDtypeStruct((2 * half, width, lanes), jnp.float32)
    outward = [(i, i + 2) for i in range(1, size - 2, 2)] + [(i, i - 2) for i in range(2, size, 2)]
    across = [(i, i + 1) for i in range(1, size - 1, 2)] + [(i + 1, i) for i in range(1, size - 1, 2)]
    far = lax.ppermute(far, "elem", outward)
    mate = pl.pallas_call(
        mate_kernel,
        out_shape=double,
        in_specs=[SMEM] + [VMEM] * WINDOWS,
        out_specs=VMEM,
        compiler_params=PARAMS,
        cost_estimate=pl.CostEstimate(flops=10**8, bytes_accessed=4 * 10**6, transcendentals=0),
    )(place, *windows)
    mate = lax.ppermute(mate, "elem", [(i, i ^ 1) for i in range(size)])
    near, here = pl.pallas_call(
        rest_kernel,
        out_shape=[slab, slab],
        in_specs=[SMEM] + [VMEM] * (WINDOWS + 1),
        out_specs=[VMEM, VMEM],
        compiler_params=PARAMS,
        cost_estimate=pl.CostEstimate(flops=hint, bytes_accessed=4 * 10**6, transcendentals=0),
    )(place, *windows, own)
    near = lax.ppermute(near + mate[half:], "elem", across)
    return here, mate[:half], far, near


def body(blocks, cols, inverse, right_side, start):
    width = start.shape[0]
    count = cols.shape[1]
    place = lax.axis_index("elem").astype(jnp.int32).reshape(1)
    out = jax.ShapeDtypeStruct(start.shape, jnp.float32)
    cols = in_hbm(cols)
    *windows, own, far, panel = pl.pallas_call(
        first_kernel,
        out_shape=applied(width, count) + [pltpu.VMEM(blocks.shape[::-1], jnp.bfloat16)],
        in_specs=[SMEM, HBM, HBM, HBM],
        out_specs=[VMEM] * (WINDOWS + 3),
        scratch_shapes=[pltpu.SMEM(cols.shape, jnp.int32), pltpu.VMEM(start.shape, jnp.float32)] + scratch(width, count),
        compiler_params=PARAMS,
    )(place, cols, in_hbm(blocks.T), in_hbm(start))
    parts = exchange(place, windows, own, far, 10**8)
    *windows, own, far, first = pl.pallas_call(
        second_kernel,
        out_shape=applied(width, count) + [out],
        in_specs=[SMEM, HBM] + [VMEM] * 8,
        out_specs=[VMEM] * (WINDOWS + 3),
        scratch_shapes=[pltpu.SMEM(cols.shape, jnp.int32)] + scratch(width, count),
        compiler_params=PARAMS,
    )(place, cols, panel, right_side, start, inverse, *parts)
    parts = exchange(place, windows, own, far, 10**10)
    adjoint, residual = pl.pallas_call(
        last_kernel,
        out_shape=[out, out],
        in_specs=[VMEM] * 7,
        out_specs=[VMEM] * 2,
        compiler_params=PARAMS,
    )(right_side, first, inverse, *parts)
    return (adjoint, residual)


def solution(mesh):
    return jax.shard_map(
        body,
        mesh=mesh,
        in_specs=(
            P("elem", None),
            P(None, "elem"),
            P(None, "elem"),
            P("rhs", "elem"),
            P("rhs", "elem"),
        ),
        out_specs=(P("rhs", "elem"), P("rhs", "elem")),
        check_vma=False,
    )
```
